256 devices in a mesh: dp: 64 (over y, z, core), mp: 4 (over x).
Axes of the slice: x: 4, y: 4, z: 8, core: 2. Of those that a mesh axis runs over, the one named last changes fastest.
Arguments:
- tokens: bfloat16 [64, 1568, 1280], P('dp', None, 'mp'), may hold values from -3 to 3
- ln_gain: float32 [1280], replicated, may hold values from 0.1 to 1.9
- w_qkv: bfloat16 [1280, 3, 1280], P(None, None, 'mp'), may hold values from -0.15625 to 0.15625
- w_out: bfloat16 [1280, 1280], P('mp'), may hold values from -0.625 to 0.625
- mask_index: int32 [64, 1176], P('dp'), may hold values from 0 to 1567, as said below
- owners: int32 [64, 1176, 1], P('dp'), may hold values from 0 to 63; in each aligned block of 1176 rows (0 to 1175, 1176 to 2351, ..., all dimensions but the last counted through in order) at most 40 rows name the same one
- pred_hidden: bfloat16 [163840, 384], P('dp'), may hold values from -6 to 6
- w_pred: bfloat16 [384, 1280], P(None, 'mp'), may hold values from -0.3125 to 0.3125
Outputs:
- grad_hidden: float32 [163840, 384], P('dp', 'mp')
- grad_proj: float32 [384, 1280], P(None, 'mp')
The draws below stay inside these ranges and needn't reach their ends.
Inputs may be any that keep to these rules, and one draw needn't show every extreme that they name: `mask_index`: each clip's row holds 1176 distinct positions t * 196 + q for all t below 8 and 147 patches q drawn for that clip. `owners`: among the rows of one index of dp, no owner is named by more than 40 rows.
All inputs are finite; a program needn't handle non-finite values.
Results may differ from the reference program's by a relative error of at most 0.0065.
Values may be sent and summed in bfloat16 or wider, within the bound.
No kernel may reach another device: no remote copies, remote signals or barrier semaphores. Data moves between devices by JAX's collectives and lax.ppermute only.
A program may use at most 64 MiB of HBM per device.

```python
import math
import jax
import jax.numpy as jnp
import numpy as np
from jax import lax

HEADS = 16
HD = 80
D = 1280
PD = 384
PATCHES = 196
TSTEPS = 8
MASKED_P = 147
CLIPS_DEV = 1
TOK = 1568
MASKED = 1176
CLIPS = 64
CAP = 40
N_DP = 64
N_MP = 4


def draw_mask_index(key, part):
    key = jax.random.fold_in(key, 7)
    keys = jax.random.split(key, CLIPS)

    def one_clip(clip_key):
        chosen = jax.random.permutation(clip_key, PATCHES)[:MASKED_P].astype(jnp.int32)
        steps = jnp.arange(TSTEPS, dtype=jnp.int32)[:, None] * PATCHES
        return (steps + chosen[None, :]).reshape(MASKED)
    return jax.vmap(one_clip)(keys).astype(jnp.int32)


def level_of(rng, extent, cuts, least, largest):
    level, own = 1.0, jax.random.fold_in(rng, 6)
    for dim, blocks in cuts:
        draws = jnp.exp(jax.random.uniform(jax.random.fold_in(own, dim), (blocks,), jnp.float32, least / len(cuts), largest / len(cuts)))
        level = level * jnp.repeat(draws, extent[dim] // blocks).reshape([-1 if axis == dim else 1 for axis in range(len(extent))])
    return level


def assign_block(rng, own, number, rows, count, top, most, lean):
    sequence = jax.random.permutation(rng, count)
    crowded, common = portions_of(count, rows * top, most, lean, True), portions_of(count, rows * top, most, lean, False)
    places = jnp.arange(count)

    def named(sizes, offset_by):
        used = int((sizes > 0).sum())
        fixed = max(1, used // 4)
        moved = fixed + (places - fixed + offset_by * (used - fixed)) % max(1, count - fixed)
        return jnp.zeros((count,), jnp.int32).at[sequence[jnp.where(places < fixed, places, moved)]].set(jnp.asarray(sizes, jnp.int32))

    sizes = jnp.where(number % 4 == 0, named(crowded, number // 4), named(common, number - number // 4 - 1))
    mixed = jax.random.permutation(jax.random.fold_in(own, 3), count)
    giver, receiver = mixed[0:count // 2 * 2:2], mixed[1:count // 2 * 2:2]
    margin = jnp.minimum(sizes[giver] - 1, most - sizes[receiver]) // 2
    margin = jnp.where((giver == sequence[0]) | (receiver == sequence[0]) | (sizes[receiver] == 0), 0, jnp.maximum(margin, 0))
    moved = jax.random.randint(jax.random.fold_in(own, 4), (count // 2,), 0, 1 << 20) % (margin + 1)
    sizes = sizes.at[giver].add(-moved).at[receiver].add(moved)
    items = jnp.searchsorted(jnp.cumsum(sizes), jnp.arange(rows * top), side="right").astype(jnp.int32)
    listing = items.reshape(top, rows).T
    listing = listing[jax.random.permutation(jax.random.fold_in(own, 1), rows)]
    offset_by = jax.random.randint(jax.random.fold_in(own, 2), (rows, 1), 0, top)
    return jnp.take_along_axis(listing, (jnp.arange(top)[None, :] + offset_by) % top, axis=1)


def portions_of(amount, total, most, skew, full):
    portions = [(1 << 20) // math.isqrt(grade ** skew) + 1 for grade in range(1, amount + 1)]
    largest = most if full else min(most, max(-(-total // amount), total * portions[0] // sum(portions)))
    least = 1 if total - largest >= amount - 1 else 0
    given, surplus = [largest] + [least] * (amount - 1), total - largest - least * (amount - 1)
    while surplus > 0:
        candidates = [i for i in range(1, amount) if given[i] < largest] or [i for i in range(1, amount) if given[i] < most]
        mass, remaining = sum([portions[i] for i in candidates]), surplus
        for i in candidates:
            extra = min(most - given[i], max(1, remaining * portions[i] // mass), surplus)
            given[i] = given[i] + extra
            surplus = surplus - extra
    return np.array(given)


def noise(key, dims, scale, reach, cuts=(), kind=jnp.bfloat16):
    result = jax.random.normal(key, dims, jnp.float32) * scale
    if len(cuts) > 0:
        result = level_of(key, dims, cuts, -0.22, 0.18) * result
    return jnp.clip(result, min=-reach, max=reach).astype(kind)


def setup_inputs(seed: int = 0) -> dict:
    seeds = jax.random.split(jax.random.key(seed), 9)
    tokens = noise(seeds[0], (CLIPS, TOK, D), 0.5, 3.0, ((0, 64), (2, 4)))
    ln_gain = jnp.clip(1.0 + 0.18 * jax.random.normal(seeds[1], (D,), jnp.float32), 0.1, 1.9)
    w_qkv = noise(seeds[2], (D, 3, D), D ** -0.5, 0.15625, ((2, 4),))
    w_out = noise(seeds[3], (D, D), (D // 16) ** -0.5, 0.625, ((0, 4),))
    mask_index = draw_mask_index(jax.random.fold_in(seeds[8], 71), 0)
    owners_keys = jax.random.split(jax.random.fold_in(seeds[5], 1), CLIPS * MASKED // (CLIPS_DEV * MASKED))
    owners_turns = jax.random.permutation(jax.random.fold_in(seeds[5], 3), CLIPS * MASKED // (CLIPS_DEV * MASKED))
    owners = jax.vmap(lambda own, number: assign_block(jax.random.fold_in(seeds[5], 2), own, number, CLIPS_DEV * MASKED, N_DP, 1, CAP, 2))(owners_keys, owners_turns).reshape((CLIPS, MASKED, 1))
    pred_hidden = noise(seeds[6], (N_DP * N_DP * CAP, PD), 1.0, 6.0, ((0, 64),))
    w_pred = noise(seeds[7], (PD, D), PD ** -0.5, 0.3125, ((1, 4),))
    return {"tokens": tokens, "ln_gain": ln_gain, "w_qkv": w_qkv, "w_out": w_out, "mask_index": mask_index, "owners": owners, "pred_hidden": pred_hidden, "w_pred": w_pred}


norm_eps = 1e-06

def normalize(x):
    mean = lax.optimization_barrier(jnp.mean(x, axis=-1, keepdims=True))
    centered = x - mean
    var = lax.optimization_barrier(jnp.mean(centered * centered, axis=-1, keepdims=True))
    return centered / jnp.sqrt(var + norm_eps)

def encode_clip(clip_tokens, ln_gain, w_qkv, w_out):
    x = clip_tokens.astype(jnp.float32)
    normed = (normalize(x) * ln_gain).astype(jnp.bfloat16)
    qkv = jnp.dot(normed, w_qkv.reshape(D, 3 * D), preferred_element_type=jnp.float32).astype(jnp.bfloat16)
    qkv = qkv.reshape(TOK, 3, HEADS, HD)

    def one_head(head):
        query = qkv[:, 0, head, :]
        key_rows = qkv[:, 1, head, :]
        value = qkv[:, 2, head, :]
        scores = jnp.dot(query, key_rows.T, preferred_element_type=jnp.float32) / jnp.sqrt(jnp.float32(HD))
        weights = jnp.exp(scores)
        probs = (weights / lax.optimization_barrier(jnp.sum(weights, axis=-1, keepdims=True))).astype(jnp.bfloat16)
        return jnp.dot(probs, value, preferred_element_type=jnp.float32).astype(jnp.bfloat16)
    heads_out = lax.map(one_head, jnp.arange(HEADS, dtype=jnp.int32))
    attended = jnp.transpose(heads_out, (1, 0, 2)).reshape(TOK, D)
    width = D // N_MP
    proj = jnp.zeros((TOK, D), jnp.float32)
    for block in range(N_MP):
        part = jnp.dot(attended[:, block * width:(block + 1) * width], w_out[block * width:(block + 1) * width, :], preferred_element_type=jnp.float32)
        proj = proj + part.astype(jnp.bfloat16).astype(jnp.float32)
    resid = x + proj
    return normalize(resid).astype(jnp.bfloat16)

def reference(tokens, ln_gain, w_qkv, w_out, mask_index, owners, pred_hidden, w_pred):
    rows_dev = CLIPS_DEV * MASKED
    own_rows = N_DP * CAP

    def per_source(carry, source):
        grad_hidden, grad_proj = carry
        clips = lax.dynamic_slice_in_dim(tokens, source * CLIPS_DEV, CLIPS_DEV, 0)
        index = lax.dynamic_slice_in_dim(mask_index, source * CLIPS_DEV, CLIPS_DEV, 0)
        owner = lax.dynamic_slice_in_dim(owners, source * CLIPS_DEV, CLIPS_DEV, 0).reshape(rows_dev)
        targets = lax.map(lambda c: encode_clip(c, ln_gain, w_qkv, w_out), clips)
        rows = jnp.take_along_axis(targets, index[:, :, None], axis=1).reshape(rows_dev, D)
        onehot = (owner[:, None] == jnp.arange(N_DP, dtype=jnp.int32)[None, :]).astype(jnp.int32)
        rank = jnp.cumsum(onehot, axis=0) - 1
        slot = lax.optimization_barrier(jnp.sum(rank * onehot, axis=1)).astype(jnp.int32)
        place = (owner * own_rows + source * CAP + slot).astype(jnp.int32)
        hidden = pred_hidden[place]
        pred = jnp.dot(hidden, w_pred, preferred_element_type=jnp.float32)
        errors = jnp.clip(pred - rows.astype(jnp.float32), -1.0, 1.0).astype(jnp.bfloat16)
        grad_proj = grad_proj + jnp.dot(hidden.T, errors, preferred_element_type=jnp.float32)
        back = jnp.dot(errors, w_pred.T, preferred_element_type=jnp.float32)
        grad_hidden = grad_hidden.at[place].set(back)
        return ((grad_hidden, grad_proj), None)
    start = (jnp.zeros((N_DP * own_rows, PD), jnp.float32), jnp.zeros((PD, D), jnp.float32))
    (grad_hidden, grad_proj), _ = lax.scan(per_source, start, jnp.arange(N_DP, dtype=jnp.int32))
    return (grad_hidden, grad_proj / MASKED)
```

```python
import functools
import math

import jax
import jax.numpy as jnp
import numpy as np
from jax import lax
from jax.experimental import pallas as pl
from jax.experimental.pallas import tpu as pltpu
from jax.sharding import PartitionSpec as P

HD = 80
LOCAL_HEADS = 4
MASKED = 1176
TOK = 1568
D = 1280
WIDTH = 320
PD = 384
N_DP = 64
N_MP = 4
CAP = 40
SLOTS = CAP // N_MP
SLOTS_PAD = 16
GROUP = 16
BLK = 352
QN = N_MP * BLK
OUT_W = PD // N_MP
EPS = 1e-06
V_SCALE = 2.0**-9
VMEM_LIMIT = 56 << 20
BF = jnp.bfloat16
F32 = jnp.float32
NT = (((1,), (1,)), ((), ()))
TN = (((0,), (0,)), ((), ()))


def one_hot(cond):
    return jnp.where(cond, 1.0, 0.0).astype(BF)


def prepare_kernel(
    m_ref, core_ref, mask_ref, owner_ref, hidden_ref, w_out_ref, w_pred_ref, col_ref, row_ref, slots_ref, weights_ref
):
    group = GROUP * SLOTS_PAD
    to = lax.broadcasted_iota(jnp.int32, (group, GROUP * CAP), 0)
    r = to & (SLOTS_PAD - 1)
    source = (to >> 4) * CAP + N_MP * r + m_ref[0]
    hot = one_hot(jnp.where(r < SLOTS, source, -1) == lax.broadcasted_iota(jnp.int32, (group, GROUP * CAP), 1))
    for g in range(N_DP // GROUP):
        rows = hidden_ref[g * GROUP * CAP : (g + 1) * GROUP * CAP, :]
        slots_ref[g * group : (g + 1) * group, :] = jnp.dot(hot, rows, preferred_element_type=F32).astype(BF)
    half = WIDTH // 2
    at = pl.ds(pl.multiple_of(core_ref[0] * half, half), half)
    weights_ref[:, :D] = w_out_ref[at, :]
    weights_ref[:, D:] = w_pred_ref[at, :]

    owner = owner_ref[...]
    tok = mask_ref[...]
    earlier = one_hot(
        lax.broadcasted_iota(jnp.int32, (MASKED, MASKED), 0)
        < lax.broadcasted_iota(jnp.int32, (MASKED, MASKED), 1)
    )
    named = lax.broadcasted_iota(jnp.int32, (N_DP, MASKED), 0) == owner
    rank = jnp.dot(one_hot(named), earlier, preferred_element_type=F32)
    slot = jnp.sum(jnp.where(named, rank, 0.0), axis=0, keepdims=True).astype(jnp.int32)
    part = slot & (N_MP - 1)
    part_named = lax.broadcasted_iota(jnp.int32, (16, MASKED), 0) == part
    before = jnp.dot(one_hot(part_named), earlier, preferred_element_type=F32)
    pos = jnp.sum(jnp.where(part_named, before, 0.0), axis=0, keepdims=True).astype(jnp.int32)
    dest = part * BLK + pos
    place = owner * SLOTS_PAD + (slot >> 2)
    sub = lax.broadcasted_iota(jnp.int32, (16, MASKED), 0)
    values = jnp.where(sub == 0, tok >> 6, 0)
    values = jnp.where(sub == 1, tok & 63, values)
    values = jnp.where(sub == 2, place >> 6, values)
    values = jnp.where(sub == 3, place & 63, values)
    values = jnp.where(sub == 4, 1, values).astype(F32).astype(BF)
    for block in range(N_MP):
        to = lax.broadcasted_iota(jnp.int32, (BLK, MASKED), 0) + block * BLK
        hot = one_hot(to == dest)
        cols = lax.dot_general(hot, values, NT, preferred_element_type=F32).astype(jnp.int32)
        used = cols[:, 4:5] > 0
        lane = lax.broadcasted_iota(jnp.int32, (BLK, 128), 1)
        tok_col = jnp.where(used, cols[:, 0:1] * 64 + cols[:, 1:2], -1)
        place_col = jnp.where(used, cols[:, 2:3] * 64 + cols[:, 3:4], -1)
        col_ref[block] = jnp.where(lane == 0, tok_col, place_col)
        rows = lax.dot_general(values, hot, NT, preferred_element_type=F32).astype(jnp.int32)
        place_row = jnp.where(rows[4:5, :] > 0, rows[2:3, :] * 64 + rows[3:4, :], -1)
        row_ref[block] = jnp.broadcast_to(place_row, (8, BLK))


def prepare(m, core, mask_index, owners, pred_hidden, w_out, w_pred):
    vmem = pl.BlockSpec(memory_space=pltpu.VMEM)
    smem = pl.BlockSpec(memory_space=pltpu.SMEM)
    return pl.pallas_call(
        prepare_kernel,
        in_specs=[smem, smem] + [vmem] * 5,
        out_specs=[vmem] * 4,
        out_shape=(
            jax.ShapeDtypeStruct((N_MP, BLK, 128), jnp.int32),
            jax.ShapeDtypeStruct((N_MP, 8, BLK), jnp.int32),
            jax.ShapeDtypeStruct((N_DP * SLOTS_PAD, PD), BF),
            jax.ShapeDtypeStruct((WIDTH // 2, D + PD), BF),
        ),
        compiler_params=pltpu.CompilerParams(vmem_limit_bytes=VMEM_LIMIT),
        name="prepare",
    )(m, core, mask_index, owners, pred_hidden, w_out, w_pred)


FIRST = 768
PARTS = ((0, FIRST), (FIRST, TOK - FIRST))
SCORE_SCALE = math.log2(math.e) / math.sqrt(HD)
Q_STEP = 704


def key_chunks(size):
    return [(start, min(256, size - start)) for start in range(0, size, 256)]


def encode_part(m, shards, gain, w_ref, col_ref, xs, xn, qkv, vaug, part, keep_query, keep_picked):
    own, right, left, opp_a, opp_b = shards
    offset, size = part

    def shard(k):
        return pl.multiple_of(((m + k) & 3) * WIDTH, WIDTH)

    xs[pl.ds(shard(0), WIDTH), :] = own[...]
    xs[pl.ds(shard(3), WIDTH), :] = right[...]
    xs[pl.ds(shard(1), WIDTH), :] = left[...]
    across = shard(2)
    xs[pl.ds(across, WIDTH // 2), :] = opp_a[...]
    xs[pl.ds(pl.multiple_of(across + WIDTH // 2, WIDTH // 2), WIDTH // 2), :] = opp_b[...]

    def rows16(i):
        return pl.ds(pl.multiple_of(i * 16, 16), 16)

    total = lax.fori_loop(
        0, D // 16, lambda i, acc: acc + xs[rows16(i), :].astype(F32), jnp.zeros((16, size), F32), unroll=2
    )
    mean = jnp.sum(total, axis=0, keepdims=True) / D

    def square(i, acc):
        centered = xs[rows16(i), :].astype(F32) - mean
        return acc + centered * centered

    squares = lax.fori_loop(0, D // 16, square, jnp.zeros((16, size), F32), unroll=2)
    rstd = lax.rsqrt(jnp.sum(squares, axis=0, keepdims=True) / D + EPS)

    def norm(i, carry):
        centered = xs[rows16(i), :].astype(F32) - mean
        xn[rows16(i), :] = (centered * rstd * gain[rows16(i), :]).astype(BF)
        return carry

    lax.fori_loop(0, D // 16, norm, 0, unroll=2)

    pad_rows = jnp.where(lax.broadcasted_iota(jnp.int32, (16, size), 0) == 0, 1.0, 0.0).astype(BF)
    for h in range(LOCAL_HEADS):
        vaug[h, HD:, :] = pad_rows
    for start, width in key_chunks(size):
        keys = pl.ds(start, width)
        for kind in range(3):
            rows = slice(kind * WIDTH, (kind + 1) * WIDTH)
            res = jnp.dot(w_ref[rows, :], xn[:, keys], preferred_element_type=F32)
            if kind < 2:
                qkv[rows, keys] = res.astype(BF)
            else:
                res = (res * V_SCALE).astype(BF)
                for h in range(LOCAL_HEADS):
                    vaug[h, :HD, keys] = res[h * HD : (h + 1) * HD, :]

    token = lax.broadcasted_iota(jnp.int32, (BLK, size), 1) + offset

    def select(k, hot):
        found = lax.dot_general(hot, qkv[:WIDTH, :], NT, preferred_element_type=F32)
        keep_query(pl.ds(pl.multiple_of(k * BLK, 16), BLK), found)

    def step(k, carry):
        select(k, one_hot(token == col_ref[(m + k) & 3][:, 0:1]))
        return carry

    hot = one_hot(token == col_ref[m][:, 0:1])
    keep_picked(lax.dot_general(hot, xs[...], NT, preferred_element_type=F32))
    select(0, hot)
    lax.fori_loop(1, N_MP, step, 0)


def first_kernel(
    m_ref, own, right, left, opp_a, opp_b, gain, w_ref, col_ref,
    key_ref, value_ref, query_ref, picked_ref, xs, xn, qkv,
):
    def keep_query(at, found):
        query_ref[at, :] = found.astype(BF)

    def keep_picked(found):
        picked_ref[...] = found.astype(BF)

    shards = (own, right, left, opp_a, opp_b)
    encode_part(
        m_ref[0], shards, gain, w_ref, col_ref, xs, xn, qkv, value_ref, PARTS[0], keep_query, keep_picked
    )
    key_ref[...] = qkv[WIDTH:, :]


def attend_kernel(
    m_ref, own, right, left, opp_a, opp_b, gain, w_ref, col_ref,
    key_first, value_first, query_first, picked_first,
    out_own, out_next, out_across, out_prev, picked_ref,
    xs, xn, qkv, vaug, qsel, heads,
):
    def keep_query(at, found):
        rows = (found + query_first[at, :].astype(F32)).astype(BF)
        for h in range(LOCAL_HEADS):
            qsel[h, at, :] = rows[:, h * HD : (h + 1) * HD]

    def keep_picked(found):
        picked_ref[...] = (found + picked_first[...].astype(F32)).astype(BF)

    shards = (own, right, left, opp_a, opp_b)
    encode_part(m_ref[0], shards, gain, w_ref, col_ref, xs, xn, qkv, vaug, PARTS[1], keep_query, keep_picked)

    def head_step(step, carry):
        h = step >> 1
        at = pl.ds(pl.multiple_of((step & 1) * Q_STEP, 16), Q_STEP)
        query = qsel[h, at, :]
        first_rows = pl.ds(pl.multiple_of(h * HD, 16), HD)
        key_rows = pl.ds(pl.multiple_of(WIDTH + h * HD, 16), HD)
        acc = jnp.zeros((Q_STEP, 96), F32)
        for keys_ref, key_at, values_ref, size in (
            (key_first, first_rows, value_first, FIRST),
            (qkv, key_rows, vaug, TOK - FIRST),
        ):
            for start, width in key_chunks(size):
                keys = pl.ds(start, width)
                scores = jnp.dot(query, keys_ref[key_at, keys], preferred_element_type=F32)
                weights = jnp.exp2(scores * SCORE_SCALE).astype(BF)
                acc = acc + lax.dot_general(weights, values_ref[h, :, keys], NT, preferred_element_type=F32)
        heads[h, at, :] = (acc[:, :HD] / acc[:, HD : HD + 1] * (1.0 / V_SCALE)).astype(BF)
        return carry

    lax.fori_loop(0, LOCAL_HEADS * QN // Q_STEP, head_step, 0)
    for k, out in enumerate((out_own, out_next, out_across, out_prev)):
        for h in range(LOCAL_HEADS):
            out[:, h * HD : (h + 1) * HD] = heads[h, k * BLK : (k + 1) * BLK, :]


def encode_first(m, shards, gain, w, cols):
    vmem = pl.BlockSpec(memory_space=pltpu.VMEM)
    return pl.pallas_call(
        first_kernel,
        in_specs=[pl.BlockSpec(memory_space=pltpu.SMEM)] + [vmem] * 8,
        out_specs=[vmem] * 4,
        out_shape=(
            jax.ShapeDtypeStruct((WIDTH, FIRST), BF),
            jax.ShapeDtypeStruct((LOCAL_HEADS, 96, FIRST), BF),
            jax.ShapeDtypeStruct((QN, WIDTH), BF),
            jax.ShapeDtypeStruct((BLK, D), BF),
        ),
        scratch_shapes=[
            pltpu.VMEM((D, FIRST), BF),
            pltpu.VMEM((D, FIRST), BF),
            pltpu.VMEM((2 * WIDTH, FIRST), BF),
        ],
        compiler_params=pltpu.CompilerParams(vmem_limit_bytes=VMEM_LIMIT),
        cost_estimate=pl.CostEstimate(flops=4_000_000_000, bytes_accessed=6_000_000, transcendentals=0),
        name="encode_first",
    )(m, *shards, gain, w, cols)


def attend(m, shards, gain, w, cols, first):
    block = jax.ShapeDtypeStruct((BLK, WIDTH), BF)
    vmem = pl.BlockSpec(memory_space=pltpu.VMEM)
    rest = TOK - FIRST
    return pl.pallas_call(
        attend_kernel,
        in_specs=[pl.BlockSpec(memory_space=pltpu.SMEM)] + [vmem] * 12,
        out_specs=[vmem] * 5,
        out_shape=(block, block, block, block, jax.ShapeDtypeStruct((BLK, D), BF)),
        scratch_shapes=[
            pltpu.VMEM((D, rest), BF),
            pltpu.VMEM((D, rest), BF),
            pltpu.VMEM((2 * WIDTH, rest), BF),
            pltpu.VMEM((LOCAL_HEADS, 96, rest), BF),
            pltpu.VMEM((LOCAL_HEADS, QN, HD), BF),
            pltpu.VMEM((LOCAL_HEADS, QN, HD), BF),
        ],
        compiler_params=pltpu.CompilerParams(vmem_limit_bytes=VMEM_LIMIT),
        cost_estimate=pl.CostEstimate(flops=16_000_000_000, bytes_accessed=8_000_000, transcendentals=9_000_000),
        name="attend",
    )(m, *shards, gain, w, cols, *first)


def head_kernel(
    m_ref, core_ref, a_own, a_prev, a_across, a_next, w_mine, w_other,
    picked, hidden_in, col_ref, grad_ref, err_ref, w_pred_ref, w_out, proj, pred,
):
    m = m_ref[0]
    core = core_ref[0]
    half = WIDTH // 2
    mine = pl.multiple_of(core * half, half)
    other = pl.multiple_of((1 - core) * half, half)
    for b in range(N_MP):
        for at, part in ((mine, w_mine), (other, w_other)):
            w_out[b, pl.ds(at, half), :] = part[b, :, :D]
            w_pred_ref[pl.ds(pl.multiple_of(b * WIDTH + at, half), half), :] = part[b, :, D:]

    hot = one_hot(lax.broadcasted_iota(jnp.int32, (BLK, N_DP * SLOTS_PAD), 1) == col_ref[m][:, 1:2])
    hidden = jnp.dot(hot, hidden_in[...], preferred_element_type=F32).astype(BF)
    for n in range(5):
        lanes = slice(n * 256, (n + 1) * 256)
        acc = jnp.dot(a_own[...], w_out[m, :, lanes], preferred_element_type=F32)
        acc = acc + jnp.dot(a_prev[...], w_out[(m + 3) & 3, :, lanes], preferred_element_type=F32)
        acc = acc + jnp.dot(a_across[...], w_out[(m + 2) & 3, :, lanes], preferred_element_type=F32)
        acc = acc + jnp.dot(a_next[...], w_out[(m + 1) & 3, :, lanes], preferred_element_type=F32)
        proj[:, lanes] = acc
        pred[:, lanes] = lax.dot_general(hidden, w_pred_ref[lanes, :], NT, preferred_element_type=F32)

    def rows(i, carry):
        at = pl.ds(pl.multiple_of(i * 16, 16), 16)
        resid = picked[at, :].astype(F32) + proj[at, :]
        mean = jnp.mean(resid, axis=-1, keepdims=True)
        centered = resid - mean
        var = jnp.mean(centered * centered, axis=-1, keepdims=True)
        target = (centered * lax.rsqrt(var + EPS)).astype(BF).astype(F32)
        err_ref[at, :] = jnp.clip(pred[at, :] - target, -1.0, 1.0).astype(BF)
        return carry

    lax.fori_loop(0, BLK // 16, rows, 0, unroll=2)
    for b in range(N_MP):
        lanes = slice(b * WIDTH, (b + 1) * WIDTH)
        grad_ref[b] = lax.dot_general(err_ref[:, lanes], hidden, TN, preferred_element_type=F32).astype(BF)


def message_kernel(m_ref, err, w_pred, row_ref, msg_ref):
    back = jnp.dot(err[...], w_pred[...], preferred_element_type=F32).astype(BF)
    place = row_ref[m_ref[0]][0:1, :]
    row_id = lax.broadcasted_iota(jnp.int32, (N_DP * 8, BLK), 0)
    owner_at = (row_id >> 3) * SLOTS_PAD
    low = row_id & 7
    lane_to = lax.broadcasted_iota(jnp.int32, (PD, 4 * 128), 1)
    feature = lax.broadcasted_iota(jnp.int32, (PD, 4 * 128), 0)
    block_lane = lane_to & 127
    first = feature == (lane_to >> 7) * OUT_W + block_lane
    spread = jnp.dot(back, one_hot(first & (block_lane < OUT_W)), preferred_element_type=F32).astype(BF)
    acc = jnp.dot(one_hot(place == owner_at + low), spread, preferred_element_type=F32)
    for i in range(3):
        piece = feature == (lane_to >> 7) * OUT_W + block_lane - OUT_W + 32 * i
        spread = jnp.dot(back, one_hot(piece & (block_lane >= OUT_W)), preferred_element_type=F32).astype(BF)
        wanted = jnp.where(low == i, owner_at + 8, jnp.where(low == i + 3, owner_at + 9, -2))
        acc = acc + jnp.dot(one_hot(place == wanted), spread, preferred_element_type=F32)
    for c in range(N_MP):
        msg_ref[c] = acc[:, c * 128 : (c + 1) * 128].astype(BF)


def predictor_head(m, core, blocks, weights, picked, hidden_in, cols):
    vmem = pl.BlockSpec(memory_space=pltpu.VMEM)
    smem = pl.BlockSpec(memory_space=pltpu.SMEM)
    return pl.pallas_call(
        head_kernel,
        in_specs=[smem, smem] + [vmem] * 9,
        out_specs=[vmem] * 3,
        out_shape=(
            jax.ShapeDtypeStruct((N_MP, WIDTH, PD), BF),
            jax.ShapeDtypeStruct((BLK, D), BF),
            jax.ShapeDtypeStruct((D, PD), BF),
        ),
        scratch_shapes=[
            pltpu.VMEM((N_MP, WIDTH, D), BF),
            pltpu.VMEM((BLK, D), F32),
            pltpu.VMEM((BLK, D), F32),
        ],
        compiler_params=pltpu.CompilerParams(vmem_limit_bytes=VMEM_LIMIT),
        cost_estimate=pl.CostEstimate(flops=2_000_000_000, bytes_accessed=9_000_000, transcendentals=0),
        name="predictor_head",
    )(m, core, *blocks, *weights, picked, hidden_in, cols)


def pack_messages(m, err, w_pred, rows):
    vmem = pl.BlockSpec(memory_space=pltpu.VMEM)
    return pl.pallas_call(
        message_kernel,
        in_specs=[pl.BlockSpec(memory_space=pltpu.SMEM)] + [vmem] * 3,
        out_specs=vmem,
        out_shape=jax.ShapeDtypeStruct((N_MP, N_DP * 8, 128), BF),
        compiler_params=pltpu.CompilerParams(vmem_limit_bytes=VMEM_LIMIT),
        cost_estimate=pl.CostEstimate(flops=2_000_000_000, bytes_accessed=3_000_000, transcendentals=0),
        name="pack_messages",
    )(m, err, w_pred, rows)


def unpack_table():
    table = np.full((8, GROUP * CAP), -1, np.int32)
    for source in range(GROUP):
        for slot in range(CAP):
            m, r = slot % N_MP, slot // N_MP
            base = m * GROUP * 8 + source * 8
            if r < 8:
                table[0, source * CAP + slot] = base + r
            else:
                for i in range(3):
                    table[1 + i, source * CAP + slot] = base + 3 * (r - 8) + i
    return table


def unpack_kernel(table_ref, in_ref, out_ref):
    row = lax.broadcasted_iota(jnp.int32, (N_MP * GROUP * 8, GROUP * CAP), 0)
    hots = [one_hot(row == table_ref[i : i + 1, :]) for i in range(4)]
    for g in range(N_DP // GROUP):
        part = jnp.concatenate([in_ref[m, g * GROUP * 8 : (g + 1) * GROUP * 8, :] for m in range(N_MP)], axis=0)
        flipped = part.astype(F32).T.astype(BF)
        lanes = slice(g * GROUP * CAP, (g + 1) * GROUP * CAP)
        main = jnp.dot(flipped[:OUT_W, :], hots[0], preferred_element_type=F32)
        for i in range(3):
            extra = jnp.dot(flipped[OUT_W:, :], hots[1 + i], preferred_element_type=F32)
            out_ref[32 * i : 32 * (i + 1), lanes] = main[32 * i : 32 * (i + 1), :] + extra


def unpack(arrived):
    return pl.pallas_call(
        unpack_kernel,
        out_shape=jax.ShapeDtypeStruct((OUT_W, N_DP * CAP), F32),
        compiler_params=pltpu.CompilerParams(vmem_limit_bytes=VMEM_LIMIT),
        name="unpack",
    )(jnp.asarray(unpack_table()), arrived)


def ring(step):
    return [(i, (i + step) % N_MP) for i in range(N_MP)]


def dp_index(y, z, core):
    return (y * 8 + z) * 2 + core


def dp_shift(dy, dz):
    return [
        (dp_index(y, z, c), dp_index((y + dy) % 4, (z + dz) % 8, c))
        for y in range(4)
        for z in range(8)
        for c in range(2)
    ]


Z_PAIR = [(i, i ^ 2) for i in range(N_DP)]
SIBLING = [(i, i ^ 1) for i in range(N_DP)]


def at(array, index):
    return lax.dynamic_index_in_dim(array, index, 0, keepdims=False)


def reduce_grad(grad, msg, m, y, core):
    halves = grad.reshape(N_MP, 2, WIDTH // 2, PD)
    kept = lax.dynamic_index_in_dim(halves, core, 1, keepdims=False)
    sent = lax.dynamic_index_in_dim(halves, 1 - core, 1, keepdims=False)
    both = kept.astype(F32) + lax.ppermute(sent, "dp", SIBLING).astype(F32)
    sends = both.astype(BF)
    total = at(both, m)
    for k in (2, 1, 3):
        total = total + lax.ppermute(at(sends, (m + k) & 3), "mp", ring(k)).astype(F32)
    total, msg = lax.optimization_barrier((total, msg))
    arrived = lax.all_to_all(msg, ("mp", "dp"), 0, 0, tiled=True)
    quarters = total.reshape(4, WIDTH // 8, PD)
    sends = quarters.astype(BF)
    total = at(quarters, y)
    for k in (2, 1, 3):
        total = total + lax.ppermute(at(sends, (y + k) & 3), "dp", dp_shift(k, 0)).astype(F32)
    total = total + lax.ppermute(total, "dp", Z_PAIR)
    send = total
    for k in (4, 2, 6):
        total = total + lax.ppermute(send, "dp", dp_shift(0, k))
    mine = total * (1.0 / MASKED)
    mine, arrived = lax.optimization_barrier((mine, arrived))
    parts = [mine] + [lax.ppermute(mine, "dp", dp_shift(k, 0)) for k in (1, 2, 3)]
    stacked = jnp.stack(parts)
    half = jnp.concatenate([at(stacked, (y - j) & 3) for j in range(4)], axis=0)
    other = lax.ppermute(half, "dp", SIBLING)
    return arrived, jnp.where(core == 0, jnp.concatenate([half, other]), jnp.concatenate([other, half]))


def per_device(tokens, ln_gain, w_qkv, w_out, mask_index, owners, pred_hidden, w_pred):
    m = lax.axis_index("mp")
    dp = lax.axis_index("dp")
    core, y = dp & 1, dp >> 4
    m_arr = m.astype(jnp.int32).reshape(1)
    core_arr = core.astype(jnp.int32).reshape(1)

    w_flat = jnp.transpose(w_qkv, (1, 2, 0)).reshape(3 * WIDTH, D)
    half = WIDTH // 2
    own = [tokens[0].T[:, start : start + size] for start, size in PARTS]
    right = [lax.ppermute(part, "mp", ring(1)) for part in own]
    left = [lax.ppermute(part, "mp", ring(3)) for part in own]

    gain = ln_gain.reshape(D, 1)
    cols, rows, slots, weights = prepare(
        m_arr, core_arr, mask_index, owners.reshape(1, MASKED), pred_hidden, w_out, w_pred.T
    )
    right[0], left[0], cols, rows, slots, weights, gain = lax.optimization_barrier(
        (right[0], left[0], cols, rows, slots, weights, gain)
    )
    slots = slots.reshape(N_DP, SLOTS_PAD, PD)
    hidden_in = lax.all_to_all(slots, "dp", 0, 0, tiled=True).reshape(N_DP * SLOTS_PAD, PD)
    opp_a = [lax.ppermute(right[0][:half], "mp", ring(1))]
    opp_b = [lax.ppermute(left[0][half:], "mp", ring(3))]
    opp_a += [lax.ppermute(right[1][:half], "mp", ring(1))]
    opp_b += [lax.ppermute(left[1][half:], "mp", ring(3))]

    opp_a[0], opp_b[0], weights = lax.optimization_barrier((opp_a[0], opp_b[0], weights))
    w_mine = lax.all_gather(weights, "mp", axis=0)
    shards = [(own[i], right[i], left[i], opp_a[i], opp_b[i]) for i in range(2)]
    first = encode_first(m_arr, shards[0], gain, w_flat, cols)
    opp_a[1], opp_b[1], hidden_in, *first = lax.optimization_barrier((opp_a[1], opp_b[1], hidden_in, *first))
    shards[1] = (own[1], right[1], left[1], opp_a[1], opp_b[1])
    a_own, to_next, to_across, to_prev, picked = attend(m_arr, shards[1], gain, w_flat, cols, first)
    a_across = lax.ppermute(to_across, "mp", ring(2))
    a_prev = lax.ppermute(to_next, "mp", ring(1))
    a_next = lax.ppermute(to_prev, "mp", ring(3))
    w_mine, a_next = lax.optimization_barrier((w_mine, a_next))
    w_other = lax.ppermute(w_mine, "dp", SIBLING)
    grad, err, w_pred_all = predictor_head(
        m_arr, core_arr, (a_own, a_prev, a_across, a_next), (w_mine, w_other), picked, hidden_in, cols
    )
    msg = pack_messages(m_arr, err, w_pred_all, rows)
    msg = msg.reshape(N_MP * N_DP, 8, 128)
    arrived, grad_proj = reduce_grad(grad, msg, m, y, core)
    grad_hidden = unpack(arrived.reshape(N_MP, N_DP * 8, 128)).T
    grad_proj = grad_proj.T
    return (grad_hidden, grad_proj)


def solution(mesh):
    placed = (
        P("dp", None, "mp"),
        P(),
        P(None, None, "mp"),
        P("mp", None),
        P("dp", None),
        P("dp", None, None),
        P("dp", None),
        P(None, "mp"),
    )
    return jax.shard_map(
        per_device,
        mesh=mesh,
        in_specs=placed,
        out_specs=(P("dp", "mp"), P(None, "mp")),
        check_vma=False,
    )
```

```python
import functools
import math

import jax
import jax.numpy as jnp
import numpy as np
from jax import lax
from jax.experimental import pallas as pl
from jax.experimental.pallas import tpu as pltpu
from jax.sharding import PartitionSpec as P

HD = 80
LOCAL_HEADS = 4
MASKED = 1176
TOK = 1568
D = 1280
WIDTH = 320
PD = 384
N_DP = 64
N_MP = 4
CAP = 40
SLOTS = CAP // N_MP
SLOTS_PAD = 16
GROUP = 16
BLK = 352
QN = N_MP * BLK
OUT_W = PD // N_MP
EPS = 1e-06
V_SCALE = 2.0**-9
VMEM_LIMIT = 56 << 20
BF = jnp.bfloat16
F32 = jnp.float32
NT = (((1,), (1,)), ((), ()))
TN = (((0,), (0,)), ((), ()))


def one_hot(cond):
    return jnp.where(cond, 1.0, 0.0).astype(BF)


def prepare_kernel(
    core_ref, mask_ref, owner_ref, w_out_ref, w_pred_ref, col_ref, row_ref, weights_ref
):
    half = WIDTH // 2
    at = pl.ds(pl.multiple_of(core_ref[0] * half, half), half)
    weights_ref[:, :D] = w_out_ref[at, :]
    weights_ref[:, D:] = w_pred_ref[at, :]

    owner = owner_ref[...]
    tok = mask_ref[...]
    earlier = one_hot(
        lax.broadcasted_iota(jnp.int32, (MASKED, MASKED), 0)
        < lax.broadcasted_iota(jnp.int32, (MASKED, MASKED), 1)
    )
    named = lax.broadcasted_iota(jnp.int32, (N_DP, MASKED), 0) == owner
    rank = jnp.dot(one_hot(named), earlier, preferred_element_type=F32)
    slot = jnp.sum(jnp.where(named, rank, 0.0), axis=0, keepdims=True).astype(jnp.int32)
    part = slot & (N_MP - 1)
    part_named = lax.broadcasted_iota(jnp.int32, (16, MASKED), 0) == part
    before = jnp.dot(one_hot(part_named), earlier, preferred_element_type=F32)
    pos = jnp.sum(jnp.where(part_named, before, 0.0), axis=0, keepdims=True).astype(jnp.int32)
    dest = part * BLK + pos
    place = owner * SLOTS_PAD + (slot >> 2)
    sub = lax.broadcasted_iota(jnp.int32, (16, MASKED), 0)
    values = jnp.where(sub == 0, tok >> 6, 0)
    values = jnp.where(sub == 1, tok & 63, values)
    values = jnp.where(sub == 2, place >> 6, values)
    values = jnp.where(sub == 3, place & 63, values)
    values = jnp.where(sub == 4, 1, values).astype(F32).astype(BF)
    for block in range(N_MP):
        to = lax.broadcasted_iota(jnp.int32, (BLK, MASKED), 0) + block * BLK
        hot = one_hot(to == dest)
        cols = lax.dot_general(hot, values, NT, preferred_element_type=F32).astype(jnp.int32)
        used = cols[:, 4:5] > 0
        lane = lax.broadcasted_iota(jnp.int32, (BLK, 128), 1)
        tok_col = jnp.where(used, cols[:, 0:1] * 64 + cols[:, 1:2], -1)
        place_col = jnp.where(used, cols[:, 2:3] * 64 + cols[:, 3:4], -1)
        col_ref[block] = jnp.where(lane == 0, tok_col, place_col)
        rows = lax.dot_general(values, hot, NT, preferred_element_type=F32).astype(jnp.int32)
        place_row = jnp.where(rows[4:5, :] > 0, rows[2:3, :] * 64 + rows[3:4, :], -1)
        row_ref[block] = jnp.broadcast_to(place_row, (8, BLK))


def prepare(core, mask_index, owners, w_out, w_pred):
    vmem = pl.BlockSpec(memory_space=pltpu.VMEM)
    return pl.pallas_call(
        prepare_kernel,
        in_specs=[pl.BlockSpec(memory_space=pltpu.SMEM)] + [vmem] * 4,
        out_specs=[vmem] * 3,
        out_shape=(
            jax.ShapeDtypeStruct((N_MP, BLK, 128), jnp.int32),
            jax.ShapeDtypeStruct((N_MP, 8, BLK), jnp.int32),
            jax.ShapeDtypeStruct((WIDTH // 2, D + PD), BF),
        ),
        compiler_params=pltpu.CompilerParams(vmem_limit_bytes=VMEM_LIMIT),
        cost_estimate=pl.CostEstimate(flops=1000, bytes_accessed=1000, transcendentals=0),
        name="prepare",
    )(core, mask_index, owners, w_out, w_pred)


def slots_kernel(m_ref, hidden_ref, out_ref):
    group = GROUP * SLOTS_PAD
    to = lax.broadcasted_iota(jnp.int32, (group, GROUP * CAP), 0)
    r = to & (SLOTS_PAD - 1)
    row = (to >> 4) * CAP + N_MP * r + m_ref[0]
    hot = one_hot(jnp.where(r < SLOTS, row, -1) == lax.broadcasted_iota(jnp.int32, (group, GROUP * CAP), 1))
    for g in range(N_DP // GROUP):
        rows = hidden_ref[g * GROUP * CAP : (g + 1) * GROUP * CAP, :]
        out_ref[g * group : (g + 1) * group, :] = jnp.dot(hot, rows, preferred_element_type=F32).astype(BF)


def pick_slots(m, pred_hidden):
    vmem = pl.BlockSpec(memory_space=pltpu.VMEM)
    return pl.pallas_call(
        slots_kernel,
        in_specs=[pl.BlockSpec(memory_space=pltpu.SMEM), vmem],
        out_specs=vmem,
        out_shape=jax.ShapeDtypeStruct((N_DP * SLOTS_PAD, PD), BF),
        compiler_params=pltpu.CompilerParams(vmem_limit_bytes=VMEM_LIMIT),
        name="pick_slots",
    )(m, pred_hidden)


SCORE_SCALE = math.log2(math.e) / math.sqrt(HD)
Q_STEP = 704


def key_chunks(size):
    return [(start, min(256, size - start)) for start in range(0, size, 256)]


def attend_kernel(
    m_ref, own, right, left, opp_a, opp_b, gain, col_ref, w_in,
    out_own, out_next, out_across, out_prev, picked_ref,
    xs, xn, qkv, vaug, qsel, heads, w_ref, sems,
):
    m = m_ref[0]
    size = TOK
    w_copy = pltpu.make_async_copy(w_in, w_ref, sems.at[0])
    w_copy.start()

    def shard(k):
        return pl.multiple_of(((m + k) & 3) * WIDTH, WIDTH)

    xs[pl.ds(shard(0), WIDTH), :] = own[...]
    xs[pl.ds(shard(3), WIDTH), :] = right[...]
    xs[pl.ds(shard(1), WIDTH), :] = left[...]
    across = shard(2)
    xs[pl.ds(across, WIDTH // 2), :] = opp_a[...]
    xs[pl.ds(pl.multiple_of(across + WIDTH // 2, WIDTH // 2), WIDTH // 2), :] = opp_b[...]

    def rows16(i):
        return pl.ds(pl.multiple_of(i * 16, 16), 16)

    total = lax.fori_loop(
        0, D // 16, lambda i, acc: acc + xs[rows16(i), :].astype(F32), jnp.zeros((16, size), F32), unroll=2
    )
    mean = jnp.sum(total, axis=0, keepdims=True) / D

    def square(i, acc):
        centered = xs[rows16(i), :].astype(F32) - mean
        return acc + centered * centered

    squares = lax.fori_loop(0, D // 16, square, jnp.zeros((16, size), F32), unroll=2)
    rstd = lax.rsqrt(jnp.sum(squares, axis=0, keepdims=True) / D + EPS)

    def norm(i, carry):
        centered = xs[rows16(i), :].astype(F32) - mean
        xn[rows16(i), :] = (centered * rstd * gain[rows16(i), :]).astype(BF)
        return carry

    lax.fori_loop(0, D // 16, norm, 0, unroll=2)

    pad_rows = jnp.where(lax.broadcasted_iota(jnp.int32, (16, size), 0) == 0, 1.0, 0.0).astype(BF)
    for h in range(LOCAL_HEADS):
        vaug[h, HD:, :] = pad_rows
    w_copy.wait()
    for start, width in key_chunks(size):
        keys = pl.ds(start, width)
        for kind in range(3):
            rows = slice(kind * WIDTH, (kind + 1) * WIDTH)
            res = jnp.dot(w_ref[rows, :], xn[:, keys], preferred_element_type=F32)
            if kind < 2:
                qkv[rows, keys] = res.astype(BF)
            else:
                res = (res * V_SCALE).astype(BF)
                for h in range(LOCAL_HEADS):
                    vaug[h, :HD, keys] = res[h * HD : (h + 1) * HD, :]

    token = lax.broadcasted_iota(jnp.int32, (BLK, size), 1)

    def select(k, hot):
        found = lax.dot_general(hot, qkv[:WIDTH, :], NT, preferred_element_type=F32)
        at = pl.ds(pl.multiple_of(k * BLK, 16), BLK)
        rows = found.astype(BF)
        for h in range(LOCAL_HEADS):
            qsel[h, at, :] = rows[:, h * HD : (h + 1) * HD]

    def step(k, carry):
        select(k, one_hot(token == col_ref[(m + k) & 3][:, 0:1]))
        return carry

    hot = one_hot(token == col_ref[m][:, 0:1])
    picked_ref[...] = lax.dot_general(hot, xs[...], NT, preferred_element_type=F32).astype(BF)
    select(0, hot)
    lax.fori_loop(1, N_MP, step, 0)

    def head_step(step, carry):
        h = step >> 1
        at = pl.ds(pl.multiple_of((step & 1) * Q_STEP, 16), Q_STEP)
        query = qsel[h, at, :]
        key_rows = pl.ds(pl.multiple_of(WIDTH + h * HD, 16), HD)
        acc = jnp.zeros((Q_STEP, 96), F32)
        for start, width in key_chunks(size):
            keys = pl.ds(start, width)
            scores = jnp.dot(query, qkv[key_rows, keys], preferred_element_type=F32)
            weights = jnp.exp2(scores * SCORE_SCALE).astype(BF)
            acc = acc + lax.dot_general(weights, vaug[h, :, keys], NT, preferred_element_type=F32)
        heads[h, at, :] = (acc[:, :HD] / acc[:, HD : HD + 1] * (1.0 / V_SCALE)).astype(BF)
        return carry

    lax.fori_loop(0, LOCAL_HEADS * QN // Q_STEP, head_step, 0)
    for k, out in enumerate((out_own, out_next, out_across, out_prev)):
        for h in range(LOCAL_HEADS):
            out[:, h * HD : (h + 1) * HD] = heads[h, k * BLK : (k + 1) * BLK, :]


def attend(m, shards, gain, w, cols):
    block = jax.ShapeDtypeStruct((BLK, WIDTH), BF)
    vmem = pl.BlockSpec(memory_space=pltpu.VMEM)
    return pl.pallas_call(
        attend_kernel,
        in_specs=[pl.BlockSpec(memory_space=pltpu.SMEM)] + [vmem] * 7 + [pl.BlockSpec(memory_space=pl.ANY)],
        out_specs=[vmem] * 5,
        out_shape=(block, block, block, block, jax.ShapeDtypeStruct((BLK, D), BF)),
        scratch_shapes=[
            pltpu.VMEM((D, TOK), BF),
            pltpu.VMEM((D, TOK), BF),
            pltpu.VMEM((2 * WIDTH, TOK), BF),
            pltpu.VMEM((LOCAL_HEADS, 96, TOK), BF),
            pltpu.VMEM((LOCAL_HEADS, QN, HD), BF),
            pltpu.VMEM((LOCAL_HEADS, QN, HD), BF),
            pltpu.VMEM((3 * WIDTH, D), BF),
            pltpu.SemaphoreType.DMA((1,)),
        ],
        compiler_params=pltpu.CompilerParams(vmem_limit_bytes=VMEM_LIMIT),
        cost_estimate=pl.CostEstimate(flops=16_000_000_000, bytes_accessed=8_000_000, transcendentals=9_000_000),
        name="attend",
    )(m, *shards, gain, cols, w)


def head_kernel(
    m_ref, a_own, a_prev, a_across, a_next, w_halves,
    picked, hidden_in, col_in, row_ref, grad_ref, msg_ref, err_ref, w_pred_ref, w_out, proj, pred, col_ref, sems,
):
    m = m_ref[0]
    half = WIDTH // 2
    copies = []
    for b in range(N_MP):
        for core in range(2):
            src, at, n = w_halves.at[core, b], core * half, 4 * b + 2 * core
            to_out, to_pred = w_out.at[b, pl.ds(at, half)], w_pred_ref.at[pl.ds(b * WIDTH + at, half)]
            copies.append(pltpu.make_async_copy(src.at[:, pl.ds(0, D)], to_out, sems.at[n]))
            copies.append(pltpu.make_async_copy(src.at[:, pl.ds(D, PD)], to_pred, sems.at[n + 1]))
    copies.append(pltpu.make_async_copy(col_in.at[m], col_ref, sems.at[16]))
    for copy in reversed(copies):
        copy.start()

    copies.pop().wait()
    hot = one_hot(lax.broadcasted_iota(jnp.int32, (BLK, N_DP * SLOTS_PAD), 1) == col_ref[:, 1:2])
    hidden = jnp.dot(hot, hidden_in[...], preferred_element_type=F32).astype(BF)
    for copy in copies:
        copy.wait()
    for n in range(5):
        lanes = slice(n * 256, (n + 1) * 256)
        acc = jnp.dot(a_own[...], w_out[m, :, lanes], preferred_element_type=F32)
        acc = acc + jnp.dot(a_prev[...], w_out[(m + 3) & 3, :, lanes], preferred_element_type=F32)
        acc = acc + jnp.dot(a_across[...], w_out[(m + 2) & 3, :, lanes], preferred_element_type=F32)
        acc = acc + jnp.dot(a_next[...], w_out[(m + 1) & 3, :, lanes], preferred_element_type=F32)
        proj[:, lanes] = acc
        pred[:, lanes] = lax.dot_general(hidden, w_pred_ref[lanes, :], NT, preferred_element_type=F32)

    def rows(i, carry):
        at = pl.ds(pl.multiple_of(i * 16, 16), 16)
        resid = picked[at, :].astype(F32) + proj[at, :]
        mean = jnp.mean(resid, axis=-1, keepdims=True)
        centered = resid - mean
        var = jnp.mean(centered * centered, axis=-1, keepdims=True)
        target = (centered * lax.rsqrt(var + EPS)).astype(BF).astype(F32)
        err_ref[at, :] = jnp.clip(pred[at, :] - target, -1.0, 1.0).astype(BF)
        return carry

    lax.fori_loop(0, BLK // 16, rows, 0, unroll=11)
    for b in range(N_MP):
        lanes = slice(b * WIDTH, (b + 1) * WIDTH)
        grad_ref[b] = lax.dot_general(err_ref[:, lanes], hidden, TN, preferred_element_type=F32).astype(BF)

    back = jnp.dot(err_ref[...], w_pred_ref[...], preferred_element_type=F32).astype(BF)
    place = row_ref[m][0:1, :]
    row_id = lax.broadcasted_iota(jnp.int32, (N_DP * 8, BLK), 0)
    owner_at = (row_id >> 3) * SLOTS_PAD
    low = row_id & 7
    lane_to = lax.broadcasted_iota(jnp.int32, (PD, 4 * 128), 1)
    feature = lax.broadcasted_iota(jnp.int32, (PD, 4 * 128), 0)
    block_lane = lane_to & 127
    first = feature == (lane_to >> 7) * OUT_W + block_lane
    spread = jnp.dot(back, one_hot(first & (block_lane < OUT_W)), preferred_element_type=F32).astype(BF)
    acc = jnp.dot(one_hot(place == owner_at + low), spread, preferred_element_type=F32)
    for i in range(3):
        piece = feature == (lane_to >> 7) * OUT_W + block_lane - OUT_W + 32 * i
        spread = jnp.dot(back, one_hot(piece & (block_lane >= OUT_W)), preferred_element_type=F32).astype(BF)
        wanted = jnp.where(low == i, owner_at + 8, jnp.where(low == i + 3, owner_at + 9, -2))
        acc = acc + jnp.dot(one_hot(place == wanted), spread, preferred_element_type=F32)
    for c in range(N_MP):
        msg_ref[c] = acc[:, c * 128 : (c + 1) * 128].astype(BF)


def predictor_head(m, blocks, weights, picked, hidden_in, cols, rows):
    vmem = pl.BlockSpec(memory_space=pltpu.VMEM)
    anywhere = pl.BlockSpec(memory_space=pl.ANY)
    return pl.pallas_call(
        head_kernel,
        in_specs=[pl.BlockSpec(memory_space=pltpu.SMEM)] + [vmem] * 4 + [anywhere, vmem, vmem, anywhere, vmem],
        out_specs=[vmem] * 2,
        out_shape=(
            jax.ShapeDtypeStruct((N_MP, WIDTH, PD), BF),
            jax.ShapeDtypeStruct((N_MP, N_DP * 8, 128), BF),
        ),
        scratch_shapes=[
            pltpu.VMEM((BLK, D), BF),
            pltpu.VMEM((D, PD), BF),
            pltpu.VMEM((N_MP, WIDTH, D), BF),
            pltpu.VMEM((BLK, D), F32),
            pltpu.VMEM((BLK, D), F32),
            pltpu.VMEM((BLK, 128), jnp.int32),
            pltpu.SemaphoreType.DMA((17,)),
        ],
        compiler_params=pltpu.CompilerParams(vmem_limit_bytes=VMEM_LIMIT),
        cost_estimate=pl.CostEstimate(flops=4_000_000_000, bytes_accessed=9_000_000, transcendentals=0),
        name="predictor_head",
    )(m, *blocks, weights, picked, hidden_in, cols, rows)


def unpack_table():
    table = np.full((8, GROUP * CAP), -1, np.int32)
    for source in range(GROUP):
        for slot in range(CAP):
            m, r = slot % N_MP, slot // N_MP
            base = m * GROUP * 8 + source * 8
            if r < 8:
                table[0, source * CAP + slot] = base + r
            else:
                for i in range(3):
                    table[1 + i, source * CAP + slot] = base + 3 * (r - 8) + i
    return table


def unpack_kernel(table_ref, in_ref, out_ref):
    row = lax.broadcasted_iota(jnp.int32, (N_MP * GROUP * 8, GROUP * CAP), 0)
    hots = [one_hot(row == table_ref[i : i + 1, :]) for i in range(4)]
    for g in range(N_DP // GROUP):
        part = jnp.concatenate([in_ref[m, g * GROUP * 8 : (g + 1) * GROUP * 8, :] for m in range(N_MP)], axis=0)
        flipped = part.astype(F32).T.astype(BF)
        lanes = slice(g * GROUP * CAP, (g + 1) * GROUP * CAP)
        main = jnp.dot(flipped[:OUT_W, :], hots[0], preferred_element_type=F32)
        for i in range(3):
            extra = jnp.dot(flipped[OUT_W:, :], hots[1 + i], preferred_element_type=F32)
            out_ref[32 * i : 32 * (i + 1), lanes] = main[32 * i : 32 * (i + 1), :] + extra


def unpack(arrived):
    return pl.pallas_call(
        unpack_kernel,
        out_shape=jax.ShapeDtypeStruct((OUT_W, N_DP * CAP), F32),
        compiler_params=pltpu.CompilerParams(vmem_limit_bytes=VMEM_LIMIT),
        name="unpack",
    )(jnp.asarray(unpack_table()), arrived)


def ring(step):
    return [(i, (i + step) % N_MP) for i in range(N_MP)]


def dp_index(y, z, core):
    return (y * 8 + z) * 2 + core


def dp_shift(dy, dz):
    return [
        (dp_index(y, z, c), dp_index((y + dy) % 4, (z + dz) % 8, c))
        for y in range(4)
        for z in range(8)
        for c in range(2)
    ]


Z_PAIR = [(i, i ^ 2) for i in range(N_DP)]
SIBLING = [(i, i ^ 1) for i in range(N_DP)]
CHIP_ROWS = [[8 * chip + i for i in range(8)] for chip in range(N_DP // 2)]


def at(array, index):
    return lax.dynamic_index_in_dim(array, index, 0, keepdims=False)


def reduce_grad(grad, msg, m, y, core):
    halves = grad.reshape(N_MP, 2, WIDTH // 2, PD)
    kept = lax.dynamic_index_in_dim(halves, core, 1, keepdims=False)
    sent = lax.dynamic_index_in_dim(halves, 1 - core, 1, keepdims=False)
    both = kept.astype(F32) + lax.ppermute(sent, "dp", SIBLING).astype(F32)
    both, msg = lax.optimization_barrier((both, msg))
    arrived = lax.all_to_all(msg, ("mp", "dp"), 0, 0, tiled=True)
    sends = both.astype(BF)
    total = at(both, m)
    for k in (2, 1, 3):
        total = total + lax.ppermute(at(sends, (m + k) & 3), "mp", ring(k)).astype(F32)
    quarters = total.reshape(4, WIDTH // 8, PD)
    sends = quarters.astype(BF)
    total = at(quarters, y)
    for k in (2, 1, 3):
        total = total + lax.ppermute(at(sends, (y + k) & 3), "dp", dp_shift(k, 0)).astype(F32)
    total = total + lax.ppermute(total, "dp", Z_PAIR)
    send = total
    for k in (4, 2, 6):
        total = total + lax.ppermute(send, "dp", dp_shift(0, k))
    mine = total * (1.0 / MASKED)
    mine, arrived = lax.optimization_barrier((mine, arrived))
    parts = [mine] + [lax.ppermute(mine, "dp", dp_shift(k, 0)) for k in (1, 2, 3)]
    stacked = jnp.stack(parts)
    half = jnp.concatenate([at(stacked, (y - j) & 3) for j in range(4)], axis=0)
    other = lax.ppermute(half, "dp", SIBLING)
    return arrived, jnp.where(core == 0, jnp.concatenate([half, other]), jnp.concatenate([other, half]))


def per_device(tokens, ln_gain, w_qkv, w_out, mask_index, owners, pred_hidden, w_pred):
    m = lax.axis_index("mp")
    dp = lax.axis_index("dp")
    core, y = dp & 1, dp >> 4
    m_arr = m.astype(jnp.int32).reshape(1)
    core_arr = core.astype(jnp.int32).reshape(1)

    w_flat = jnp.transpose(w_qkv, (1, 2, 0)).reshape(3 * WIDTH, D)
    half = WIDTH // 2
    own = tokens[0].T
    right = lax.ppermute(own, "mp", ring(1))
    left = lax.ppermute(own, "mp", ring(3))

    slots = pick_slots(m_arr, pred_hidden).reshape(N_DP, SLOTS_PAD, PD)
    gain = ln_gain.reshape(D, 1)
    cols, rows, weights = prepare(core_arr, mask_index, owners.reshape(1, MASKED), w_out, w_pred.T)
    right, left, slots, cols, rows, weights, gain = lax.optimization_barrier(
        (right, left, slots, cols, rows, weights, gain)
    )
    hidden_in = lax.all_to_all(slots, "dp", 0, 0, tiled=True).reshape(N_DP * SLOTS_PAD, PD)
    opp_a = lax.ppermute(right[:half], "mp", ring(1))
    opp_b = lax.ppermute(left[half:], "mp", ring(3))
    opp_a, opp_b, weights = lax.optimization_barrier((opp_a, opp_b, weights))
    w_all = lax.all_gather(weights, ("dp", "mp"), axis=0, axis_index_groups=CHIP_ROWS)
    w_all = w_all.reshape(2, N_MP, half, D + PD)
    a_own, to_next, to_across, to_prev, picked = attend(
        m_arr, (own, right, left, opp_a, opp_b), gain, w_flat, cols
    )
    a_across = lax.ppermute(to_across, "mp", ring(2))
    a_prev = lax.ppermute(to_next, "mp", ring(1))
    a_next = lax.ppermute(to_prev, "mp", ring(3))
    grad, msg = predictor_head(
        m_arr, (a_own, a_prev, a_across, a_next), w_all, picked, hidden_in, cols, rows
    )
    msg = msg.reshape(N_MP * N_DP, 8, 128)
    arrived, grad_proj = reduce_grad(grad, msg, m, y, core)
    grad_hidden = unpack(arrived.reshape(N_MP, N_DP * 8, 128)).T
    grad_proj = grad_proj.T
    return (grad_hidden, grad_proj)


def solution(mesh):
    placed = (
        P("dp", None, "mp"),
        P(),
        P(None, None, "mp"),
        P("mp", None),
        P("dp", None),
        P("dp", None, None),
        P("dp", None),
        P(None, "mp"),
    )
    return jax.shard_map(
        per_device,
        mesh=mesh,
        in_specs=placed,
        out_specs=(P("dp", "mp"), P(None, "mp")),
        check_vma=False,
    )
```

```python
import functools
import math

import jax
import jax.numpy as jnp
import numpy as np
from jax import lax
from jax.experimental import pallas as pl
from jax.experimental.pallas import tpu as pltpu
from jax.sharding import PartitionSpec as P

HD = 80
LOCAL_HEADS = 4
MASKED = 1176
TOK = 1568
D = 1280
WIDTH = 320
PD = 384
N_DP = 64
N_MP = 4
CAP = 40
SLOTS = CAP // N_MP
SLOTS_PAD = 16
GROUP = 16
BLK = 352
QN = N_MP * BLK
OUT_W = PD // N_MP
EPS = 1e-06
V_SCALE = 2.0**-9
VMEM_LIMIT = 56 << 20
BF = jnp.bfloat16
F32 = jnp.float32
NT = (((1,), (1,)), ((), ()))
TN = (((0,), (0,)), ((), ()))


def one_hot(cond):
    return jnp.where(cond, 1.0, 0.0).astype(BF)


def prepare_kernel(
    core_ref, mask_ref, owner_ref, w_out_ref, w_pred_ref, gain_ref, col_ref, row_ref, weights_ref, gain_col_ref
):
    gain_col_ref[...] = jnp.broadcast_to(gain_ref[...], (8, D)).T
    half = WIDTH // 2
    at = pl.ds(pl.multiple_of(core_ref[0] * half, half), half)
    weights_ref[:, :D] = w_out_ref[at, :]
    weights_ref[:, D:] = w_pred_ref[at, :]

    owner = owner_ref[...]
    tok = mask_ref[...]
    earlier = one_hot(
        lax.broadcasted_iota(jnp.int32, (MASKED, MASKED), 0)
        < lax.broadcasted_iota(jnp.int32, (MASKED, MASKED), 1)
    )
    named = lax.broadcasted_iota(jnp.int32, (N_DP, MASKED), 0) == owner
    rank = jnp.dot(one_hot(named), earlier, preferred_element_type=F32)
    slot = jnp.sum(jnp.where(named, rank, 0.0), axis=0, keepdims=True).astype(jnp.int32)
    part = slot & (N_MP - 1)
    part_named = lax.broadcasted_iota(jnp.int32, (16, MASKED), 0) == part
    before = jnp.dot(one_hot(part_named), earlier, preferred_element_type=F32)
    pos = jnp.sum(jnp.where(part_named, before, 0.0), axis=0, keepdims=True).astype(jnp.int32)
    dest = part * BLK + pos
    place = owner * SLOTS_PAD + (slot >> 2)
    sub = lax.broadcasted_iota(jnp.int32, (16, MASKED), 0)
    values = jnp.where(sub == 0, tok >> 6, 0)
    values = jnp.where(sub == 1, tok & 63, values)
    values = jnp.where(sub == 2, place >> 6, values)
    values = jnp.where(sub == 3, place & 63, values)
    values = jnp.where(sub == 4, 1, values).astype(F32).astype(BF)
    for block in range(N_MP):
        to = lax.broadcasted_iota(jnp.int32, (BLK, MASKED), 0) + block * BLK
        hot = one_hot(to == dest)
        cols = lax.dot_general(hot, values, NT, preferred_element_type=F32).astype(jnp.int32)
        used = cols[:, 4:5] > 0
        lane = lax.broadcasted_iota(jnp.int32, (BLK, 128), 1)
        tok_col = jnp.where(used, cols[:, 0:1] * 64 + cols[:, 1:2], -1)
        place_col = jnp.where(used, cols[:, 2:3] * 64 + cols[:, 3:4], -1)
        col_ref[block] = jnp.where(lane == 0, tok_col, place_col)
        rows = lax.dot_general(values, hot, NT, preferred_element_type=F32).astype(jnp.int32)
        place_row = jnp.where(rows[4:5, :] > 0, rows[2:3, :] * 64 + rows[3:4, :], -1)
        row_ref[block] = jnp.broadcast_to(place_row, (8, BLK))


def prepare(core, mask_index, owners, w_out, w_pred, gain):
    vmem = pl.BlockSpec(memory_space=pltpu.VMEM)
    return pl.pallas_call(
        prepare_kernel,
        in_specs=[pl.BlockSpec(memory_space=pltpu.SMEM)] + [vmem] * 5,
        out_specs=[vmem] * 4,
        out_shape=(
            jax.ShapeDtypeStruct((N_MP, BLK, 128), jnp.int32),
            jax.ShapeDtypeStruct((N_MP, 8, BLK), jnp.int32),
            jax.ShapeDtypeStruct((WIDTH // 2, D + PD), BF),
            jax.ShapeDtypeStruct((D, 8), F32),
        ),
        compiler_params=pltpu.CompilerParams(vmem_limit_bytes=VMEM_LIMIT),
        cost_estimate=pl.CostEstimate(flops=1000, bytes_accessed=1000, transcendentals=0),
        name="prepare",
    )(core, mask_index, owners, w_out, w_pred, gain)


def slots_kernel(m_ref, hidden_ref, out_ref):
    group = GROUP * SLOTS_PAD
    to = lax.broadcasted_iota(jnp.int32, (group, GROUP * CAP), 0)
    r = to & (SLOTS_PAD - 1)
    row = (to >> 4) * CAP + N_MP * r + m_ref[0]
    hot = one_hot(jnp.where(r < SLOTS, row, -1) == lax.broadcasted_iota(jnp.int32, (group, GROUP * CAP), 1))
    for g in range(N_DP // GROUP):
        rows = hidden_ref[g * GROUP * CAP : (g + 1) * GROUP * CAP, :]
        out_ref[g * group : (g + 1) * group, :] = jnp.dot(hot, rows, preferred_element_type=F32).astype(BF)


def pick_slots(m, pred_hidden):
    vmem = pl.BlockSpec(memory_space=pltpu.VMEM)
    return pl.pallas_call(
        slots_kernel,
        in_specs=[pl.BlockSpec(memory_space=pltpu.SMEM), vmem],
        out_specs=vmem,
        out_shape=jax.ShapeDtypeStruct((N_DP * SLOTS_PAD, PD), BF),
        compiler_params=pltpu.CompilerParams(vmem_limit_bytes=VMEM_LIMIT),
        name="pick_slots",
    )(m, pred_hidden)


SCORE_SCALE = math.log2(math.e) / math.sqrt(HD)


def key_chunks(size):
    return [(start, min(256, size - start)) for start in range(0, size, 256)]


def attend_kernel(
    m_ref, own, right, left, opp_a, opp_b, gain, col_ref, w_in,
    out_own, out_next, out_across, out_prev, picked_ref,
    xs, xn, qkv, vaug, qsel, heads, w_ref, sems,
):
    m = m_ref[0]
    size = TOK
    w_copy = pltpu.make_async_copy(w_in, w_ref, sems.at[0])
    w_copy.start()

    def shard(k):
        return pl.multiple_of(((m + k) & 3) * WIDTH, WIDTH)

    xs[pl.ds(shard(0), WIDTH), :] = own[...]
    xs[pl.ds(shard(3), WIDTH), :] = right[...]
    xs[pl.ds(shard(1), WIDTH), :] = left[...]
    across = shard(2)
    xs[pl.ds(across, WIDTH // 2), :] = opp_a[...]
    xs[pl.ds(pl.multiple_of(across + WIDTH // 2, WIDTH // 2), WIDTH // 2), :] = opp_b[...]

    def rows16(i):
        return pl.ds(pl.multiple_of(i * 16, 16), 16)

    total = jnp.dot(jnp.ones((16, D), BF), xs[...], preferred_element_type=F32)
    mean = total[0:1, :] / D

    def square(i, acc):
        centered = xs[rows16(i), :].astype(F32) - mean
        return acc + centered * centered

    squares = lax.fori_loop(0, D // 16, square, jnp.zeros((16, size), F32), unroll=8)
    rstd = lax.rsqrt(jnp.sum(squares, axis=0, keepdims=True) / D + EPS)

    def norm(i, carry):
        centered = xs[rows16(i), :].astype(F32) - mean
        xn[rows16(i), :] = (centered * rstd * gain[rows16(i), 0:1]).astype(BF)
        return carry

    lax.fori_loop(0, D // 16, norm, 0, unroll=8)

    pad_rows = jnp.where(lax.broadcasted_iota(jnp.int32, (16, size), 0) == 0, 1.0, 0.0).astype(BF)
    for h in range(LOCAL_HEADS):
        vaug[h, HD:, :] = pad_rows
    w_copy.wait()
    for start, width in key_chunks(size):
        keys = pl.ds(start, width)
        for kind in range(3):
            rows = slice(kind * WIDTH, (kind + 1) * WIDTH)
            res = jnp.dot(w_ref[rows, :], xn[:, keys], preferred_element_type=F32)
            if kind < 2:
                qkv[rows, keys] = res.astype(BF)
            else:
                res = (res * V_SCALE).astype(BF)
                for h in range(LOCAL_HEADS):
                    vaug[h, :HD, keys] = res[h * HD : (h + 1) * HD, :]

    token = lax.broadcasted_iota(jnp.int32, (BLK, size), 1)

    def select(k, hot):
        found = lax.dot_general(hot, qkv[:WIDTH, :], NT, preferred_element_type=F32)
        at = pl.ds(pl.multiple_of(k * BLK, 16), BLK)
        rows = found.astype(BF)
        for h in range(LOCAL_HEADS):
            qsel[h, at, :] = rows[:, h * HD : (h + 1) * HD]

    def step(k, carry):
        select(k, one_hot(token == col_ref[(m + k) & 3][:, 0:1]))
        return carry

    hot = one_hot(token == col_ref[m][:, 0:1])
    picked_ref[...] = lax.dot_general(hot, xs[...], NT, preferred_element_type=F32).astype(BF)
    select(0, hot)
    lax.fori_loop(1, N_MP, step, 0)

    def head_step(h, carry):
        query = qsel[h]
        key_rows = pl.ds(pl.multiple_of(WIDTH + h * HD, 16), HD)
        acc = jnp.zeros((QN, 96), F32)
        for start, width in key_chunks(size):
            keys = pl.ds(start, width)
            scores = jnp.dot(query, qkv[key_rows, keys], preferred_element_type=F32)
            weights = jnp.exp2(scores * SCORE_SCALE).astype(BF)
            acc = acc + lax.dot_general(weights, vaug[h, :, keys], NT, preferred_element_type=F32)
        heads[h] = (acc[:, :HD] / acc[:, HD : HD + 1] * (1.0 / V_SCALE)).astype(BF)
        return carry

    lax.fori_loop(0, LOCAL_HEADS, head_step, 0)
    for k, out in enumerate((out_own, out_next, out_across, out_prev)):
        for h in range(LOCAL_HEADS):
            out[:, h * HD : (h + 1) * HD] = heads[h, k * BLK : (k + 1) * BLK, :]


def attend(m, shards, gain, w, cols):
    block = jax.ShapeDtypeStruct((BLK, WIDTH), BF)
    vmem = pl.BlockSpec(memory_space=pltpu.VMEM)
    return pl.pallas_call(
        attend_kernel,
        in_specs=[pl.BlockSpec(memory_space=pltpu.SMEM)] + [vmem] * 7 + [pl.BlockSpec(memory_space=pl.ANY)],
        out_specs=[vmem] * 5,
        out_shape=(block, block, block, block, jax.ShapeDtypeStruct((BLK, D), BF)),
        scratch_shapes=[
            pltpu.VMEM((D, TOK), BF),
            pltpu.VMEM((D, TOK), BF),
            pltpu.VMEM((2 * WIDTH, TOK), BF),
            pltpu.VMEM((LOCAL_HEADS, 96, TOK), BF),
            pltpu.VMEM((LOCAL_HEADS, QN, HD), BF),
            pltpu.VMEM((LOCAL_HEADS, QN, HD), BF),
            pltpu.VMEM((3 * WIDTH, D), BF),
            pltpu.SemaphoreType.DMA((1,)),
        ],
        compiler_params=pltpu.CompilerParams(vmem_limit_bytes=VMEM_LIMIT),
        cost_estimate=pl.CostEstimate(flops=16_000_000_000, bytes_accessed=8_000_000, transcendentals=9_000_000),
        name="attend",
    )(m, *shards, gain, cols, w)


def head_kernel(
    m_ref, a_own, a_prev, a_across, a_next, w_halves,
    picked, hidden_in, col_in, row_ref, grad_ref, msg_ref, err_ref, w_pred_ref, w_out, proj, pred, col_ref, sems,
):
    m = m_ref[0]
    half = WIDTH // 2
    copies = []
    for b in range(N_MP):
        for core in range(2):
            src, at, n = w_halves.at[core, b], core * half, 4 * b + 2 * core
            to_out, to_pred = w_out.at[b, pl.ds(at, half)], w_pred_ref.at[pl.ds(b * WIDTH + at, half)]
            copies.append(pltpu.make_async_copy(src.at[:, pl.ds(0, D)], to_out, sems.at[n]))
            copies.append(pltpu.make_async_copy(src.at[:, pl.ds(D, PD)], to_pred, sems.at[n + 1]))
    copies.append(pltpu.make_async_copy(col_in.at[m], col_ref, sems.at[16]))
    for copy in reversed(copies):
        copy.start()

    copies.pop().wait()
    hot = one_hot(lax.broadcasted_iota(jnp.int32, (BLK, N_DP * SLOTS_PAD), 1) == col_ref[:, 1:2])
    hidden = jnp.dot(hot, hidden_in[...], preferred_element_type=F32).astype(BF)
    for copy in copies:
        copy.wait()
    for n in range(5):
        lanes = slice(n * 256, (n + 1) * 256)
        acc = jnp.dot(a_own[...], w_out[m, :, lanes], preferred_element_type=F32)
        acc = acc + jnp.dot(a_prev[...], w_out[(m + 3) & 3, :, lanes], preferred_element_type=F32)
        acc = acc + jnp.dot(a_across[...], w_out[(m + 2) & 3, :, lanes], preferred_element_type=F32)
        acc = acc + jnp.dot(a_next[...], w_out[(m + 1) & 3, :, lanes], preferred_element_type=F32)
        proj[:, lanes] = acc
        pred[:, lanes] = lax.dot_general(hidden, w_pred_ref[lanes, :], NT, preferred_element_type=F32)

    def rows(i, carry):
        at = pl.ds(pl.multiple_of(i * 16, 16), 16)
        resid = picked[at, :].astype(F32) + proj[at, :]
        mean = jnp.mean(resid, axis=-1, keepdims=True)
        centered = resid - mean
        var = jnp.mean(centered * centered, axis=-1, keepdims=True)
        target = (centered * lax.rsqrt(var + EPS)).astype(BF).astype(F32)
        err_ref[at, :] = jnp.clip(pred[at, :] - target, -1.0, 1.0).astype(BF)
        return carry

    lax.fori_loop(0, BLK // 16, rows, 0, unroll=11)
    for b in range(N_MP):
        lanes = slice(b * WIDTH, (b + 1) * WIDTH)
        grad_ref[b] = lax.dot_general(err_ref[:, lanes], hidden, TN, preferred_element_type=F32).astype(BF)

    back = jnp.dot(err_ref[...], w_pred_ref[...], preferred_element_type=F32).astype(BF)
    place = row_ref[m][0:1, :]
    row_id = lax.broadcasted_iota(jnp.int32, (N_DP * 8, BLK), 0)
    owner_at = (row_id >> 3) * SLOTS_PAD
    low = row_id & 7
    lane_to = lax.broadcasted_iota(jnp.int32, (PD, 4 * 128), 1)
    feature = lax.broadcasted_iota(jnp.int32, (PD, 4 * 128), 0)
    block_lane = lane_to & 127
    first = feature == (lane_to >> 7) * OUT_W + block_lane
    spread = jnp.dot(back, one_hot(first & (block_lane < OUT_W)), preferred_element_type=F32).astype(BF)
    acc = jnp.dot(one_hot(place == owner_at + low), spread, preferred_element_type=F32)
    for i in range(3):
        piece = feature == (lane_to >> 7) * OUT_W + block_lane - OUT_W + 32 * i
        spread = jnp.dot(back, one_hot(piece & (block_lane >= OUT_W)), preferred_element_type=F32).astype(BF)
        wanted = jnp.where(low == i, owner_at + 8, jnp.where(low == i + 3, owner_at + 9, -2))
        acc = acc + jnp.dot(one_hot(place == wanted), spread, preferred_element_type=F32)
    for c in range(N_MP):
        msg_ref[c] = acc[:, c * 128 : (c + 1) * 128].astype(BF)


def predictor_head(m, blocks, weights, picked, hidden_in, cols, rows):
    vmem = pl.BlockSpec(memory_space=pltpu.VMEM)
    anywhere = pl.BlockSpec(memory_space=pl.ANY)
    return pl.pallas_call(
        head_kernel,
        in_specs=[pl.BlockSpec(memory_space=pltpu.SMEM)] + [vmem] * 4 + [anywhere, vmem, vmem, anywhere, vmem],
        out_specs=[vmem] * 2,
        out_shape=(
            jax.ShapeDtypeStruct((N_MP, WIDTH, PD), BF),
            jax.ShapeDtypeStruct((N_MP, N_DP * 8, 128), BF),
        ),
        scratch_shapes=[
            pltpu.VMEM((BLK, D), BF),
            pltpu.VMEM((D, PD), BF),
            pltpu.VMEM((N_MP, WIDTH, D), BF),
            pltpu.VMEM((BLK, D), F32),
            pltpu.VMEM((BLK, D), F32),
            pltpu.VMEM((BLK, 128), jnp.int32),
            pltpu.SemaphoreType.DMA((17,)),
        ],
        compiler_params=pltpu.CompilerParams(vmem_limit_bytes=VMEM_LIMIT),
        cost_estimate=pl.CostEstimate(flops=4_000_000_000, bytes_accessed=9_000_000, transcendentals=0),
        name="predictor_head",
    )(m, *blocks, weights, picked, hidden_in, cols, rows)


def unpack_table():
    table = np.full((8, GROUP * CAP), -1, np.int32)
    for source in range(GROUP):
        for slot in range(CAP):
            m, r = slot % N_MP, slot // N_MP
            base = m * GROUP * 8 + source * 8
            if r < 8:
                table[0, source * CAP + slot] = base + r
            else:
                for i in range(3):
                    table[1 + i, source * CAP + slot] = base + 3 * (r - 8) + i
    return table


def unpack_kernel(table_ref, in_ref, out_ref):
    row = lax.broadcasted_iota(jnp.int32, (N_MP * GROUP * 8, GROUP * CAP), 0)
    hots = [one_hot(row == table_ref[i : i + 1, :]) for i in range(4)]
    for g in range(N_DP // GROUP):
        part = jnp.concatenate([in_ref[m, g * GROUP * 8 : (g + 1) * GROUP * 8, :] for m in range(N_MP)], axis=0)
        flipped = part.astype(F32).T.astype(BF)
        lanes = slice(g * GROUP * CAP, (g + 1) * GROUP * CAP)
        main = jnp.dot(flipped[:OUT_W, :], hots[0], preferred_element_type=F32)
        for i in range(3):
            extra = jnp.dot(flipped[OUT_W:, :], hots[1 + i], preferred_element_type=F32)
            out_ref[32 * i : 32 * (i + 1), lanes] = main[32 * i : 32 * (i + 1), :] + extra


def unpack(arrived):
    return pl.pallas_call(
        unpack_kernel,
        out_shape=jax.ShapeDtypeStruct((OUT_W, N_DP * CAP), F32),
        compiler_params=pltpu.CompilerParams(vmem_limit_bytes=VMEM_LIMIT),
        name="unpack",
    )(jnp.asarray(unpack_table()), arrived)


def ring(step):
    return [(i, (i + step) % N_MP) for i in range(N_MP)]


def dp_index(y, z, core):
    return (y * 8 + z) * 2 + core


def dp_shift(dy, dz):
    return [
        (dp_index(y, z, c), dp_index((y + dy) % 4, (z + dz) % 8, c))
        for y in range(4)
        for z in range(8)
        for c in range(2)
    ]


Z_PAIR = [(i, i ^ 2) for i in range(N_DP)]
SIBLING = [(i, i ^ 1) for i in range(N_DP)]
CHIP_ROWS = [[8 * chip + i for i in range(8)] for chip in range(N_DP // 2)]


def at(array, index):
    return lax.dynamic_index_in_dim(array, index, 0, keepdims=False)


def reduce_grad(grad, msg, m, y, core):
    halves = grad.reshape(N_MP, 2, WIDTH // 2, PD)
    kept = lax.dynamic_index_in_dim(halves, core, 1, keepdims=False)
    sent = lax.dynamic_index_in_dim(halves, 1 - core, 1, keepdims=False)
    both = kept.astype(F32) + lax.ppermute(sent, "dp", SIBLING).astype(F32)
    both, msg = lax.optimization_barrier((both, msg))
    arrived = lax.all_to_all(msg, ("mp", "dp"), 0, 0, tiled=True)
    sends = both.astype(BF)
    total = at(both, m)
    for k in (2, 1, 3):
        total = total + lax.ppermute(at(sends, (m + k) & 3), "mp", ring(k)).astype(F32)
    quarters = total.reshape(4, WIDTH // 8, PD)
    sends = quarters.astype(BF)
    total = at(quarters, y)
    for k in (2, 1, 3):
        total = total + lax.ppermute(at(sends, (y + k) & 3), "dp", dp_shift(k, 0)).astype(F32)
    total = total + lax.ppermute(total, "dp", Z_PAIR)
    send = total
    for k in (4, 2, 6):
        total = total + lax.ppermute(send, "dp", dp_shift(0, k))
    mine = total * (1.0 / MASKED)
    mine, arrived = lax.optimization_barrier((mine, arrived))
    parts = [mine] + [lax.ppermute(mine, "dp", dp_shift(k, 0)) for k in (1, 2, 3)]
    stacked = jnp.stack(parts)
    half = jnp.concatenate([at(stacked, (y - j) & 3) for j in range(4)], axis=0)
    other = lax.ppermute(half, "dp", SIBLING)
    return arrived, jnp.where(core == 0, jnp.concatenate([half, other]), jnp.concatenate([other, half]))


def per_device(tokens, ln_gain, w_qkv, w_out, mask_index, owners, pred_hidden, w_pred):
    m = lax.axis_index("mp")
    dp = lax.axis_index("dp")
    core, y = dp & 1, dp >> 4
    m_arr = m.astype(jnp.int32).reshape(1)
    core_arr = core.astype(jnp.int32).reshape(1)

    w_flat = jnp.transpose(w_qkv, (1, 2, 0)).reshape(3 * WIDTH, D)
    half = WIDTH // 2
    own = tokens[0].T
    right = lax.ppermute(own, "mp", ring(1))
    left = lax.ppermute(own, "mp", ring(3))

    slots = pick_slots(m_arr, pred_hidden).reshape(N_DP, SLOTS_PAD, PD)
    cols, rows, weights, gain = prepare(
        core_arr, mask_index, owners.reshape(1, MASKED), w_out, w_pred.T, ln_gain.reshape(1, D)
    )
    right, left, slots, cols, rows, weights, gain = lax.optimization_barrier(
        (right, left, slots, cols, rows, weights, gain)
    )
    hidden_in = lax.all_to_all(slots, "dp", 0, 0, tiled=True).reshape(N_DP * SLOTS_PAD, PD)
    opp_a = lax.ppermute(right[:half], "mp", ring(1))
    opp_b = lax.ppermute(left[half:], "mp", ring(3))
    opp_a, opp_b, weights = lax.optimization_barrier((opp_a, opp_b, weights))
    w_all = lax.all_gather(weights, ("dp", "mp"), axis=0, axis_index_groups=CHIP_ROWS)
    w_all = w_all.reshape(2, N_MP, half, D + PD)
    a_own, to_next, to_across, to_prev, picked = attend(
        m_arr, (own, right, left, opp_a, opp_b), gain, w_flat, cols
    )
    a_across = lax.ppermute(to_across, "mp", ring(2))
    a_prev = lax.ppermute(to_next, "mp", ring(1))
    a_next = lax.ppermute(to_prev, "mp", ring(3))
    grad, msg = predictor_head(
        m_arr, (a_own, a_prev, a_across, a_next), w_all, picked, hidden_in, cols, rows
    )
    msg = msg.reshape(N_MP * N_DP, 8, 128)
    arrived, grad_proj = reduce_grad(grad, msg, m, y, core)
    grad_hidden = unpack(arrived.reshape(N_MP, N_DP * 8, 128)).T
    grad_proj = grad_proj.T
    return (grad_hidden, grad_proj)


def solution(mesh):
    placed = (
        P("dp", None, "mp"),
        P(),
        P(None, None, "mp"),
        P("mp", None),
        P("dp", None),
        P("dp", None, None),
        P("dp", None),
        P(None, "mp"),
    )
    return jax.shard_map(
        per_device,
        mesh=mesh,
        in_specs=placed,
        out_specs=(P("dp", "mp"), P(None, "mp")),
        check_vma=False,
    )
```

```python
import functools
import math

import jax
import jax.numpy as jnp
import numpy as np
from jax import lax
from jax.experimental import pallas as pl
from jax.experimental.pallas import tpu as pltpu
from jax.sharding import PartitionSpec as P

HD = 80
LOCAL_HEADS = 4
MASKED = 1176
TOK = 1568
D = 1280
WIDTH = 320
PD = 384
N_DP = 64
N_MP = 4
CAP = 40
SLOTS = CAP // N_MP
SLOTS_PAD = 16
GROUP = 16
BLK = 352
QN = N_MP * BLK
OUT_W = PD // N_MP
EPS = 1e-06
V_SCALE = 2.0**-9
VMEM_LIMIT = 56 << 20
BF = jnp.bfloat16
F32 = jnp.float32
NT = (((1,), (1,)), ((), ()))
TN = (((0,), (0,)), ((), ()))


def one_hot(cond):
    return jnp.where(cond, 1.0, 0.0).astype(BF)


def prepare_kernel(
    core_ref, mask_ref, owner_ref, w_out_ref, w_pred_ref, gain_ref, col_ref, row_ref, weights_ref, gain_col_ref
):
    gain_col_ref[...] = jnp.broadcast_to(gain_ref[...], (8, D)).T
    half = WIDTH // 2
    at = pl.ds(pl.multiple_of(core_ref[0] * half, half), half)
    weights_ref[:, :D] = w_out_ref[at, :]
    weights_ref[:, D:] = w_pred_ref[at, :]

    owner = owner_ref[...]
    tok = mask_ref[...]
    earlier = one_hot(
        lax.broadcasted_iota(jnp.int32, (MASKED, MASKED), 0)
        < lax.broadcasted_iota(jnp.int32, (MASKED, MASKED), 1)
    )
    named = lax.broadcasted_iota(jnp.int32, (N_DP, MASKED), 0) == owner
    rank = jnp.dot(one_hot(named), earlier, preferred_element_type=F32)
    slot = jnp.sum(jnp.where(named, rank, 0.0), axis=0, keepdims=True).astype(jnp.int32)
    part = slot & (N_MP - 1)
    part_named = lax.broadcasted_iota(jnp.int32, (16, MASKED), 0) == part
    before = jnp.dot(one_hot(part_named), earlier, preferred_element_type=F32)
    pos = jnp.sum(jnp.where(part_named, before, 0.0), axis=0, keepdims=True).astype(jnp.int32)
    dest = part * BLK + pos
    place = owner * SLOTS_PAD + (slot >> 2)
    sub = lax.broadcasted_iota(jnp.int32, (16, MASKED), 0)
    values = jnp.where(sub == 0, tok >> 6, 0)
    values = jnp.where(sub == 1, tok & 63, values)
    values = jnp.where(sub == 2, place >> 6, values)
    values = jnp.where(sub == 3, place & 63, values)
    values = jnp.where(sub == 4, 1, values).astype(F32).astype(BF)
    for block in range(N_MP):
        to = lax.broadcasted_iota(jnp.int32, (BLK, MASKED), 0) + block * BLK
        hot = one_hot(to == dest)
        cols = lax.dot_general(hot, values, NT, preferred_element_type=F32).astype(jnp.int32)
        used = cols[:, 4:5] > 0
        lane = lax.broadcasted_iota(jnp.int32, (BLK, 128), 1)
        tok_col = jnp.where(used, cols[:, 0:1] * 64 + cols[:, 1:2], -1)
        place_col = jnp.where(used, cols[:, 2:3] * 64 + cols[:, 3:4], -1)
        col_ref[block] = jnp.where(lane == 0, tok_col, place_col)
        rows = lax.dot_general(values, hot, NT, preferred_element_type=F32).astype(jnp.int32)
        place_row = jnp.where(rows[4:5, :] > 0, rows[2:3, :] * 64 + rows[3:4, :], -1)
        row_ref[block] = jnp.broadcast_to(place_row, (8, BLK))


def prepare(core, mask_index, owners, w_out, w_pred, gain):
    vmem = pl.BlockSpec(memory_space=pltpu.VMEM)
    return pl.pallas_call(
        prepare_kernel,
        in_specs=[pl.BlockSpec(memory_space=pltpu.SMEM)] + [vmem] * 5,
        out_specs=[vmem] * 4,
        out_shape=(
            jax.ShapeDtypeStruct((N_MP, BLK, 128), jnp.int32),
            jax.ShapeDtypeStruct((N_MP, 8, BLK), jnp.int32),
            jax.ShapeDtypeStruct((WIDTH // 2, D + PD), BF),
            jax.ShapeDtypeStruct((D, 8), F32),
        ),
        compiler_params=pltpu.CompilerParams(vmem_limit_bytes=VMEM_LIMIT),
        cost_estimate=pl.CostEstimate(flops=1000, bytes_accessed=1000, transcendentals=0),
        name="prepare",
    )(core, mask_index, owners, w_out, w_pred, gain)


def slots_kernel(m_ref, hidden_ref, out_ref):
    group = GROUP * SLOTS_PAD
    to = lax.broadcasted_iota(jnp.int32, (group, GROUP * CAP), 0)
    r = to & (SLOTS_PAD - 1)
    row = (to >> 4) * CAP + N_MP * r + m_ref[0]
    hot = one_hot(jnp.where(r < SLOTS, row, -1) == lax.broadcasted_iota(jnp.int32, (group, GROUP * CAP), 1))
    for g in range(N_DP // GROUP):
        rows = hidden_ref[g * GROUP * CAP : (g + 1) * GROUP * CAP, :]
        out_ref[g * group : (g + 1) * group, :] = jnp.dot(hot, rows, preferred_element_type=F32).astype(BF)


def pick_slots(m, pred_hidden):
    vmem = pl.BlockSpec(memory_space=pltpu.VMEM)
    return pl.pallas_call(
        slots_kernel,
        in_specs=[pl.BlockSpec(memory_space=pltpu.SMEM), vmem],
        out_specs=vmem,
        out_shape=jax.ShapeDtypeStruct((N_DP * SLOTS_PAD, PD), BF),
        compiler_params=pltpu.CompilerParams(vmem_limit_bytes=VMEM_LIMIT),
        name="pick_slots",
    )(m, pred_hidden)


SCORE_SCALE = math.log2(math.e) / math.sqrt(HD)


def key_chunks(size):
    return [(start, min(256, size - start)) for start in range(0, size, 256)]


def attend_kernel(
    m_ref, own, right, left, opp_a, opp_b, gain, col_ref, w_in,
    out_own, out_next, out_across, out_prev, picked_ref,
    xs, xn, qkv, vaug, qsel, heads, w_ref, sems,
):
    m = m_ref[0]
    size = TOK
    w_copy = pltpu.make_async_copy(w_in, w_ref, sems.at[0])
    w_copy.start()

    def shard(k):
        return pl.multiple_of(((m + k) & 3) * WIDTH, WIDTH)

    xs[pl.ds(shard(0), WIDTH), :] = own[...]
    xs[pl.ds(shard(3), WIDTH), :] = right[...]
    xs[pl.ds(shard(1), WIDTH), :] = left[...]
    across = shard(2)
    xs[pl.ds(across, WIDTH // 2), :] = opp_a[...]
    xs[pl.ds(pl.multiple_of(across + WIDTH // 2, WIDTH // 2), WIDTH // 2), :] = opp_b[...]

    def rows16(i):
        return pl.ds(pl.multiple_of(i * 16, 16), 16)

    total = jnp.dot(jnp.ones((16, D), BF), xs[...], preferred_element_type=F32)
    mean = total[0:1, :] / D

    def square(i, acc):
        centered = xs[rows16(i), :].astype(F32) - mean
        return acc + centered * centered

    squares = lax.fori_loop(0, D // 16, square, jnp.zeros((16, size), F32), unroll=8)
    rstd = lax.rsqrt(jnp.sum(squares, axis=0, keepdims=True) / D + EPS)

    def norm(i, carry):
        centered = xs[rows16(i), :].astype(F32) - mean
        xn[rows16(i), :] = (centered * rstd * gain[rows16(i), 0:1]).astype(BF)
        return carry

    lax.fori_loop(0, D // 16, norm, 0, unroll=8)

    pad_rows = jnp.where(lax.broadcasted_iota(jnp.int32, (16, size), 0) == 0, 1.0, 0.0).astype(BF)
    for h in range(LOCAL_HEADS):
        vaug[h, HD:, :] = pad_rows
    w_copy.wait()
    for start, width in key_chunks(size):
        keys = pl.ds(start, width)
        for kind in range(3):
            rows = slice(kind * WIDTH, (kind + 1) * WIDTH)
            res = jnp.dot(w_ref[rows, :], xn[:, keys], preferred_element_type=F32)
            if kind < 2:
                qkv[rows, keys] = res.astype(BF)
            else:
                res = (res * V_SCALE).astype(BF)
                for h in range(LOCAL_HEADS):
                    vaug[h, :HD, keys] = res[h * HD : (h + 1) * HD, :]

    token = lax.broadcasted_iota(jnp.int32, (BLK, size), 1)

    def select(k, hot):
        found = lax.dot_general(hot, qkv[:WIDTH, :], NT, preferred_element_type=F32)
        at = pl.ds(pl.multiple_of(k * BLK, 16), BLK)
        rows = found.astype(BF)
        for h in range(LOCAL_HEADS):
            qsel[h, at, :] = rows[:, h * HD : (h + 1) * HD]

    def step(k, carry):
        select(k, one_hot(token == col_ref[(m + k) & 3][:, 0:1]))
        return carry

    hot = one_hot(token == col_ref[m][:, 0:1])
    picked_ref[...] = lax.dot_general(hot, xs[...], NT, preferred_element_type=F32).astype(BF)
    select(0, hot)
    lax.fori_loop(1, N_MP, step, 0)

    def head_step(h, carry):
        query = qsel[h]
        key_rows = pl.ds(pl.multiple_of(WIDTH + h * HD, 16), HD)
        acc = jnp.zeros((QN, 96), F32)
        for start, width in key_chunks(size):
            keys = pl.ds(start, width)
            scores = jnp.dot(query, qkv[key_rows, keys], preferred_element_type=F32)
            weights = jnp.exp2(scores * SCORE_SCALE).astype(BF)
            acc = acc + lax.dot_general(weights, vaug[h, :, keys], NT, preferred_element_type=F32)
        heads[h] = (acc[:, :HD] / acc[:, HD : HD + 1] * (1.0 / V_SCALE)).astype(BF)
        return carry

    lax.fori_loop(0, LOCAL_HEADS, head_step, 0)
    for k, out in enumerate((out_own, out_next, out_across, out_prev)):
        for h in range(LOCAL_HEADS):
            out[:, h * HD : (h + 1) * HD] = heads[h, k * BLK : (k + 1) * BLK, :]


def attend(m, shards, gain, w, cols):
    block = jax.ShapeDtypeStruct((BLK, WIDTH), BF)
    vmem = pl.BlockSpec(memory_space=pltpu.VMEM)
    return pl.pallas_call(
        attend_kernel,
        in_specs=[pl.BlockSpec(memory_space=pltpu.SMEM)] + [vmem] * 7 + [pl.BlockSpec(memory_space=pl.ANY)],
        out_specs=[vmem] * 5,
        out_shape=(block, block, block, block, jax.ShapeDtypeStruct((BLK, D), BF)),
        scratch_shapes=[
            pltpu.VMEM((D, TOK), BF),
            pltpu.VMEM((D, TOK), BF),
            pltpu.VMEM((2 * WIDTH, TOK), BF),
            pltpu.VMEM((LOCAL_HEADS, 96, TOK), BF),
            pltpu.VMEM((LOCAL_HEADS, QN, HD), BF),
            pltpu.VMEM((LOCAL_HEADS, QN, HD), BF),
            pltpu.VMEM((3 * WIDTH, D), BF),
            pltpu.SemaphoreType.DMA((1,)),
        ],
        compiler_params=pltpu.CompilerParams(vmem_limit_bytes=VMEM_LIMIT),
        cost_estimate=pl.CostEstimate(flops=16_000_000_000, bytes_accessed=8_000_000, transcendentals=9_000_000),
        name="attend",
    )(m, *shards, gain, cols, w)


def head_kernel(
    m_ref, core_ref, a_own, a_prev, a_across, a_next, w_halves,
    picked, hidden_in, col_in, row_ref, keep_ref, send_ref, msg_ref, grad_ref, err_ref, w_pred_ref, w_out, proj, pred, col_ref, sems,
):
    m = m_ref[0]
    half = WIDTH // 2
    copies = []
    for b in range(N_MP):
        for core in range(2):
            src, at, n = w_halves.at[core, b], core * half, 4 * b + 2 * core
            to_out, to_pred = w_out.at[b, pl.ds(at, half)], w_pred_ref.at[pl.ds(b * WIDTH + at, half)]
            copies.append(pltpu.make_async_copy(src.at[:, pl.ds(0, D)], to_out, sems.at[n]))
            copies.append(pltpu.make_async_copy(src.at[:, pl.ds(D, PD)], to_pred, sems.at[n + 1]))
    copies.append(pltpu.make_async_copy(col_in.at[m], col_ref, sems.at[16]))
    for copy in reversed(copies):
        copy.start()

    copies.pop().wait()
    hot = one_hot(lax.broadcasted_iota(jnp.int32, (BLK, N_DP * SLOTS_PAD), 1) == col_ref[:, 1:2])
    hidden = jnp.dot(hot, hidden_in[...], preferred_element_type=F32).astype(BF)
    for copy in copies:
        copy.wait()
    for n in range(5):
        lanes = slice(n * 256, (n + 1) * 256)
        acc = jnp.dot(a_own[...], w_out[m, :, lanes], preferred_element_type=F32)
        acc = acc + jnp.dot(a_prev[...], w_out[(m + 3) & 3, :, lanes], preferred_element_type=F32)
        acc = acc + jnp.dot(a_across[...], w_out[(m + 2) & 3, :, lanes], preferred_element_type=F32)
        acc = acc + jnp.dot(a_next[...], w_out[(m + 1) & 3, :, lanes], preferred_element_type=F32)
        proj[:, lanes] = acc
        pred[:, lanes] = lax.dot_general(hidden, w_pred_ref[lanes, :], NT, preferred_element_type=F32)

    def rows(i, carry):
        at = pl.ds(pl.multiple_of(i * 16, 16), 16)
        resid = picked[at, :].astype(F32) + proj[at, :]
        mean = jnp.mean(resid, axis=-1, keepdims=True)
        centered = resid - mean
        var = jnp.mean(centered * centered, axis=-1, keepdims=True)
        target = (centered * lax.rsqrt(var + EPS)).astype(BF).astype(F32)
        err_ref[at, :] = jnp.clip(pred[at, :] - target, -1.0, 1.0).astype(BF)
        return carry

    lax.fori_loop(0, BLK // 16, rows, 0, unroll=11)
    for b in range(N_MP):
        lanes = slice(b * WIDTH, (b + 1) * WIDTH)
        grad_ref[b] = lax.dot_general(err_ref[:, lanes], hidden, TN, preferred_element_type=F32).astype(BF)
        keep_ref[b] = grad_ref[b, pl.ds(pl.multiple_of(core_ref[0] * half, half), half), :]
        send_ref[b] = grad_ref[b, pl.ds(pl.multiple_of((1 - core_ref[0]) * half, half), half), :]

    back = jnp.dot(err_ref[...], w_pred_ref[...], preferred_element_type=F32).astype(BF)
    place = row_ref[m][0:1, :]
    row_id = lax.broadcasted_iota(jnp.int32, (N_DP * 8, BLK), 0)
    owner_at = (row_id >> 3) * SLOTS_PAD
    low = row_id & 7
    lane_to = lax.broadcasted_iota(jnp.int32, (PD, 4 * 128), 1)
    feature = lax.broadcasted_iota(jnp.int32, (PD, 4 * 128), 0)
    block_lane = lane_to & 127
    first = feature == (lane_to >> 7) * OUT_W + block_lane
    spread = jnp.dot(back, one_hot(first & (block_lane < OUT_W)), preferred_element_type=F32).astype(BF)
    acc = jnp.dot(one_hot(place == owner_at + low), spread, preferred_element_type=F32)
    for i in range(3):
        piece = feature == (lane_to >> 7) * OUT_W + block_lane - OUT_W + 32 * i
        spread = jnp.dot(back, one_hot(piece & (block_lane >= OUT_W)), preferred_element_type=F32).astype(BF)
        wanted = jnp.where(low == i, owner_at + 8, jnp.where(low == i + 3, owner_at + 9, -2))
        acc = acc + jnp.dot(one_hot(place == wanted), spread, preferred_element_type=F32)
    for c in range(N_MP):
        msg_ref[c] = acc[:, c * 128 : (c + 1) * 128].astype(BF)


def predictor_head(m, core, blocks, weights, picked, hidden_in, cols, rows):
    vmem = pl.BlockSpec(memory_space=pltpu.VMEM)
    anywhere = pl.BlockSpec(memory_space=pl.ANY)
    return pl.pallas_call(
        head_kernel,
        in_specs=[pl.BlockSpec(memory_space=pltpu.SMEM)] * 2 + [vmem] * 4 + [anywhere, vmem, vmem, anywhere, vmem],
        out_specs=[vmem] * 3,
        out_shape=(
            jax.ShapeDtypeStruct((N_MP, WIDTH // 2, PD), BF),
            jax.ShapeDtypeStruct((N_MP, WIDTH // 2, PD), BF),
            jax.ShapeDtypeStruct((N_MP, N_DP * 8, 128), BF),
        ),
        scratch_shapes=[
            pltpu.VMEM((N_MP, WIDTH, PD), BF),
            pltpu.VMEM((BLK, D), BF),
            pltpu.VMEM((D, PD), BF),
            pltpu.VMEM((N_MP, WIDTH, D), BF),
            pltpu.VMEM((BLK, D), F32),
            pltpu.VMEM((BLK, D), F32),
            pltpu.VMEM((BLK, 128), jnp.int32),
            pltpu.SemaphoreType.DMA((17,)),
        ],
        compiler_params=pltpu.CompilerParams(vmem_limit_bytes=VMEM_LIMIT),
        cost_estimate=pl.CostEstimate(flops=4_000_000_000, bytes_accessed=9_000_000, transcendentals=0),
        name="predictor_head",
    )(m, core, *blocks, weights, picked, hidden_in, cols, rows)


def unpack_table():
    table = np.full((8, GROUP * CAP), -1, np.int32)
    for source in range(GROUP):
        for slot in range(CAP):
            m, r = slot % N_MP, slot // N_MP
            base = m * GROUP * 8 + source * 8
            if r < 8:
                table[0, source * CAP + slot] = base + r
            else:
                for i in range(3):
                    table[1 + i, source * CAP + slot] = base + 3 * (r - 8) + i
    return table


def unpack_kernel(table_ref, in_ref, out_ref):
    row = lax.broadcasted_iota(jnp.int32, (N_MP * GROUP * 8, GROUP * CAP), 0)
    hots = [one_hot(row == table_ref[i : i + 1, :]) for i in range(4)]
    for g in range(N_DP // GROUP):
        part = jnp.concatenate([in_ref[m, g * GROUP * 8 : (g + 1) * GROUP * 8, :] for m in range(N_MP)], axis=0)
        flipped = part.astype(F32).T.astype(BF)
        lanes = slice(g * GROUP * CAP, (g + 1) * GROUP * CAP)
        main = jnp.dot(flipped[:OUT_W, :], hots[0], preferred_element_type=F32)
        for i in range(3):
            extra = jnp.dot(flipped[OUT_W:, :], hots[1 + i], preferred_element_type=F32)
            out_ref[32 * i : 32 * (i + 1), lanes] = main[32 * i : 32 * (i + 1), :] + extra


def unpack(arrived):
    return pl.pallas_call(
        unpack_kernel,
        out_shape=jax.ShapeDtypeStruct((OUT_W, N_DP * CAP), F32),
        compiler_params=pltpu.CompilerParams(vmem_limit_bytes=VMEM_LIMIT),
        name="unpack",
    )(jnp.asarray(unpack_table()), arrived)


def ring(step):
    return [(i, (i + step) % N_MP) for i in range(N_MP)]


def dp_index(y, z, core):
    return (y * 8 + z) * 2 + core


def dp_shift(dy, dz):
    return [
        (dp_index(y, z, c), dp_index((y + dy) % 4, (z + dz) % 8, c))
        for y in range(4)
        for z in range(8)
        for c in range(2)
    ]


Z_PAIR = [(i, i ^ 2) for i in range(N_DP)]
SIBLING = [(i, i ^ 1) for i in range(N_DP)]
CHIP_ROWS = [[8 * chip + i for i in range(8)] for chip in range(N_DP // 2)]


def at(array, index):
    return lax.dynamic_index_in_dim(array, index, 0, keepdims=False)


def reduce_grad(kept, sent, msg, m, y, core):
    both = kept.astype(F32) + lax.ppermute(sent, "dp", SIBLING).astype(F32)
    both, msg = lax.optimization_barrier((both, msg))
    arrived = lax.all_to_all(msg, ("mp", "dp"), 0, 0, tiled=True)
    sends = both.astype(BF)
    total = at(both, m)
    for k in (2, 1, 3):
        total = total + lax.ppermute(at(sends, (m + k) & 3), "mp", ring(k)).astype(F32)
    quarters = total.reshape(4, WIDTH // 8, PD)
    sends = quarters.astype(BF)
    total = at(quarters, y)
    for k in (2, 1, 3):
        total = total + lax.ppermute(at(sends, (y + k) & 3), "dp", dp_shift(k, 0)).astype(F32)
    total = total + lax.ppermute(total, "dp", Z_PAIR)
    send = total
    for k in (4, 2, 6):
        total = total + lax.ppermute(send, "dp", dp_shift(0, k))
    mine = total * (1.0 / MASKED)
    mine, arrived = lax.optimization_barrier((mine, arrived))
    parts = [mine] + [lax.ppermute(mine, "dp", dp_shift(k, 0)) for k in (1, 2, 3)]
    stacked = jnp.stack(parts)
    half = jnp.concatenate([at(stacked, (y - j) & 3) for j in range(4)], axis=0)
    other = lax.ppermute(half, "dp", SIBLING)
    return arrived, jnp.where(core == 0, jnp.concatenate([half, other]), jnp.concatenate([other, half]))


def per_device(tokens, ln_gain, w_qkv, w_out, mask_index, owners, pred_hidden, w_pred):
    m = lax.axis_index("mp")
    dp = lax.axis_index("dp")
    core, y = dp & 1, dp >> 4
    m_arr = m.astype(jnp.int32).reshape(1)
    core_arr = core.astype(jnp.int32).reshape(1)

    w_flat = jnp.transpose(w_qkv, (1, 2, 0)).reshape(3 * WIDTH, D)
    half = WIDTH // 2
    own = tokens[0].T
    right = lax.ppermute(own, "mp", ring(1))
    left = lax.ppermute(own, "mp", ring(3))

    slots = pick_slots(m_arr, pred_hidden).reshape(N_DP, SLOTS_PAD, PD)
    cols, rows, weights, gain = prepare(
        core_arr, mask_index, owners.reshape(1, MASKED), w_out, w_pred.T, ln_gain.reshape(1, D)
    )
    right, left, slots, cols, rows, weights, gain = lax.optimization_barrier(
        (right, left, slots, cols, rows, weights, gain)
    )
    hidden_in = lax.all_to_all(slots, "dp", 0, 0, tiled=True).reshape(N_DP * SLOTS_PAD, PD)
    opp_a = lax.ppermute(right[:half], "mp", ring(1))
    opp_b = lax.ppermute(left[half:], "mp", ring(3))
    opp_a, opp_b, weights = lax.optimization_barrier((opp_a, opp_b, weights))
    w_all = lax.all_gather(weights, ("dp", "mp"), axis=0, axis_index_groups=CHIP_ROWS)
    w_all = w_all.reshape(2, N_MP, half, D + PD)
    a_own, to_next, to_across, to_prev, picked = attend(
        m_arr, (own, right, left, opp_a, opp_b), gain, w_flat, cols
    )
    a_across = lax.ppermute(to_across, "mp", ring(2))
    a_prev = lax.ppermute(to_next, "mp", ring(1))
    a_next = lax.ppermute(to_prev, "mp", ring(3))
    kept, sent, msg = predictor_head(
        m_arr, core_arr, (a_own, a_prev, a_across, a_next), w_all, picked, hidden_in, cols, rows
    )
    msg = msg.reshape(N_MP * N_DP, 8, 128)
    arrived, grad_proj = reduce_grad(kept, sent, msg, m, y, core)
    grad_hidden = unpack(arrived.reshape(N_MP, N_DP * 8, 128)).T
    grad_proj = grad_proj.T
    return (grad_hidden, grad_proj)


def solution(mesh):
    placed = (
        P("dp", None, "mp"),
        P(),
        P(None, None, "mp"),
        P("mp", None),
        P("dp", None),
        P("dp", None, None),
        P("dp", None),
        P(None, "mp"),
    )
    return jax.shard_map(
        per_device,
        mesh=mesh,
        in_specs=placed,
        out_specs=(P("dp", "mp"), P(None, "mp")),
        check_vma=False,
    )
```
